32 devices in a mesh: dp: 8 (over y, x, core), fsdp: 4 (over z).
Axes of the slice: x: 2, y: 2, z: 4, core: 2. Of those that a mesh axis runs over, the one named last changes fastest.
Arguments:
- tokens: bfloat16 [32768, 384], P(('dp', 'fsdp')), may hold values from -6 to 6
- cotangent: bfloat16 [32768, 384], P(('dp', 'fsdp')), may hold values from -6 to 6
- prefix_len: int32 [32], P(('dp', 'fsdp')), may hold values from 64 to 256, as said below
- valid_len: int32 [32], P(('dp', 'fsdp')), may hold values from 512 to 1024, as said below
- qkv_weight: float32 [2, 384, 1152], P(None, 'fsdp'), may hold values from -0.3125 to 0.3125
- qkv_first: float32 [2, 384, 1152], P(None, 'fsdp'), may hold values from -256 to 256
- qkv_second: float32 [2, 384, 1152], P(None, 'fsdp'), may hold values from 655.36 to 5242.88
- proj_weight: float32 [2, 384, 384], P(None, 'fsdp'), may hold values from -6 to 6
- proj_first: float32 [2, 384, 384], P(None, 'fsdp'), may hold values from -6 to 6
- proj_second: float32 [2, 384, 384], P(None, 'fsdp'), may hold values from 0.64 to 5.12
- up_weight: float32 [2, 384, 1536], P(None, 'fsdp'), may hold values from -0.3125 to 0.3125
- up_first: float32 [2, 384, 1536], P(None, 'fsdp'), may hold values from -32 to 32
- up_second: float32 [2, 384, 1536], P(None, 'fsdp'), may hold values from 9.8304 to 81.92
- down_weight: float32 [2, 1536, 384], P(None, 'fsdp'), may hold values from -0.15625 to 0.15625
- down_first: float32 [2, 1536, 384], P(None, 'fsdp'), may hold values from -64 to 64
- down_second: float32 [2, 1536, 384], P(None, 'fsdp'), may hold values from 40.96 to 327.68
- norm_gains: float32 [2, 2, 384], P(None, None, 'fsdp'), may hold values from 0.5 to 1.5
- gains_first: float32 [2, 2, 384], P(None, None, 'fsdp'), may hold values from -256 to 256
- gains_second: float32 [2, 2, 384], P(None, None, 'fsdp'), may hold values from 655.36 to 5242.88
Outputs:
- block_out: bfloat16 [32768, 384], P(('dp', 'fsdp'))
- tokens_grad: bfloat16 [32768, 384], P(('dp', 'fsdp'))
- qkv_first_new: float32 [2, 384, 1152], P(None, 'fsdp')
- qkv_second_new: float32 [2, 384, 1152], P(None, 'fsdp')
- qkv_new: float32 [2, 384, 1152], P(None, 'fsdp')
- proj_first_new: float32 [2, 384, 384], P(None, 'fsdp')
- proj_second_new: float32 [2, 384, 384], P(None, 'fsdp')
- proj_new: float32 [2, 384, 384], P(None, 'fsdp')
- up_first_new: float32 [2, 384, 1536], P(None, 'fsdp')
- up_second_new: float32 [2, 384, 1536], P(None, 'fsdp')
- up_new: float32 [2, 384, 1536], P(None, 'fsdp')
- down_first_new: float32 [2, 1536, 384], P(None, 'fsdp')
- down_second_new: float32 [2, 1536, 384], P(None, 'fsdp')
- down_new: float32 [2, 1536, 384], P(None, 'fsdp')
- gains_first_new: float32 [2, 2, 384], P(None, None, 'fsdp')
- gains_second_new: float32 [2, 2, 384], P(None, None, 'fsdp')
- gains_new: float32 [2, 2, 384], P(None, None, 'fsdp')
The draws below stay inside these ranges and needn't reach their ends.
Inputs may be any that keep to these rules, and one draw needn't show every extreme that they name: `prefix_len`: every sequence has a prefix shorter than its valid length; some sequence has a prefix of 256 tokens. `valid_len`: some sequence has no padding.
All inputs are finite; a program needn't handle non-finite values.
Results may differ from the reference program's by a relative error of at most 0.025.
The reference program's roundings to bfloat16 on the way count: a program that leaves them out, or rounds other values in their place, can miss the bound.
Values may be sent and summed in bfloat16 or wider, within the bound.
A program may use at most 192 MiB of HBM per device.

```python
import math
import jax
import jax.numpy as jnp
from jax import lax

D = 384
HEADS = 6
HEAD_DIM = 64
FF = 1536
SEQ = 1024
LAYERS = 2
STEP_COUNT = 7
SEQS = 32
TOKENS = 32768


def ranged_draw(key, salt, low_end, high_end):
    values = jax.random.randint(jax.random.fold_in(key, salt), (SEQS,), low_end, high_end + 1, dtype=jnp.int32)
    chosen = jax.random.randint(jax.random.fold_in(key, salt + 1), (), 0, SEQS, dtype=jnp.int32)
    places = jnp.arange(SEQS, dtype=jnp.int32)
    values = jnp.where(places == chosen, high_end, values)
    return jnp.where(places == (chosen + 1) % SEQS, low_end, values)


def draw_prefix_len(key, part):
    return ranged_draw(key, 101, max(SEQ // 16, 1), SEQ // 4)


def draw_valid_len(key, part):
    return ranged_draw(key, 211, SEQ // 2, SEQ)


def block_levels(key, extent, cuts, smallest, high):
    loudness, own = 1.0, jax.random.fold_in(key, 6)
    for dim, blocks in cuts:
        steps = jnp.exp(jax.random.uniform(jax.random.fold_in(own, dim), (blocks,), jnp.float32, smallest / len(cuts), high / len(cuts)))
        loudness = loudness * jnp.repeat(steps, extent[dim] // blocks).reshape([-1 if axis == dim else 1 for axis in range(len(extent))])
    return loudness


def gaussian(stream_key, shape, scale, most, cuts=(), kind=jnp.bfloat16):
    drawn = scale * jax.random.normal(stream_key, shape, jnp.float32)
    if cuts:
        drawn = drawn * block_levels(stream_key, shape, cuts, -0.22, 0.18)
    return jnp.clip(drawn, -most, most).astype(kind)


def setup_inputs(seed: int = 0) -> dict:
    key_of = jax.random.split(jax.random.key(seed), 20)
    return {
        "tokens": gaussian(key_of[0], (TOKENS, D), 1.0, 6.0, ((0, 32),)),
        "cotangent": gaussian(key_of[1], (TOKENS, D), 1.0, 6.0, ((0, 32),)),
        "prefix_len": draw_prefix_len(jax.random.fold_in(key_of[19], 71), 0),
        "valid_len": draw_valid_len(jax.random.fold_in(key_of[19], 71), 0),
        "qkv_weight": gaussian(key_of[4], (LAYERS, D, 3 * D), D ** -0.5, 0.3125, ((1, 4),), jnp.float32),
        "qkv_first": gaussian(key_of[5], (LAYERS, D, 3 * D), (0.22 * TOKENS ** 0.5), 256.0, ((1, 4),), jnp.float32),
        "qkv_second": jnp.clip(jnp.exp(math.log(5242.88) - 2.0794415 * jax.random.uniform(key_of[6], (LAYERS, D, 3 * D), jnp.float32) ** block_levels(key_of[6], (LAYERS, D, 3 * D), ((1, 4),), -0.2, 0.2)), 655.36, 5242.88),
        "proj_weight": gaussian(key_of[7], (LAYERS, D, D), (max(4 * D // SEQ, 1)) ** -0.5, 6.0, ((1, 4),), jnp.float32),
        "proj_first": gaussian(key_of[8], (LAYERS, D, D), (0.22 * SEQS ** 0.5), 6.0, ((1, 4),), jnp.float32),
        "proj_second": jnp.clip(jnp.exp(math.log(5.12) - 2.0794415 * jax.random.uniform(key_of[9], (LAYERS, D, D), jnp.float32) ** block_levels(key_of[9], (LAYERS, D, D), ((1, 4),), -0.2, 0.2)), 0.64, 5.12),
        "up_weight": gaussian(key_of[10], (LAYERS, D, FF), D ** -0.5, 0.3125, ((1, 4),), jnp.float32),
        "up_first": gaussian(key_of[11], (LAYERS, D, FF), (0.0275 * TOKENS ** 0.5), 32.0, ((1, 4),), jnp.float32),
        "up_second": jnp.clip(jnp.exp(math.log(81.92) - 2.1202635 * jax.random.uniform(key_of[12], (LAYERS, D, FF), jnp.float32) ** block_levels(key_of[12], (LAYERS, D, FF), ((1, 4),), -0.2, 0.2)), 9.8304, 81.92),
        "down_weight": gaussian(key_of[13], (LAYERS, FF, D), FF ** -0.5, 0.15625, ((1, 4),), jnp.float32),
        "down_first": gaussian(key_of[14], (LAYERS, FF, D), (0.055 * TOKENS ** 0.5), 64.0, ((1, 4),), jnp.float32),
        "down_second": jnp.clip(jnp.exp(math.log(327.68) - 2.0794415 * jax.random.uniform(key_of[15], (LAYERS, FF, D), jnp.float32) ** block_levels(key_of[15], (LAYERS, FF, D), ((1, 4),), -0.2, 0.2)), 40.96, 327.68),
        "norm_gains": jnp.clip(1.0 + 0.1 * jax.random.normal(key_of[16], (LAYERS, 2, D), jnp.float32), 0.5, 1.5),
        "gains_first": gaussian(key_of[17], (LAYERS, 2, D), (0.22 * TOKENS ** 0.5), 256.0, ((2, 4),), jnp.float32),
        "gains_second": jnp.clip(jnp.exp(math.log(5242.88) - 2.0794415 * jax.random.uniform(key_of[18], (LAYERS, 2, D), jnp.float32) ** block_levels(key_of[18], (LAYERS, 2, D), ((2, 4),), -0.2, 0.2)), 655.36, 5242.88),
    }


@jax.custom_vjp
def low(v):
    return lax.optimization_barrier(v.astype(jnp.bfloat16)).astype(jnp.float32)

@jax.custom_vjp
def low_back(v):
    return v

def low_keep(v):
    return (low(v), None)

def low_pass(kept, grad):
    return (grad,)

def back_keep(v):
    return (v, None)

def back_low(kept, grad):
    return (low(grad),)
low.defvjp(low_keep, low_pass)
low_back.defvjp(back_keep, back_low)
NEG_FILL = -1e+30
EPS_NORM = 1e-05
EPS_ADAM = 1e-08
BETA_ONE = 0.9
BETA_TWO = 0.99
PRECISE = lax.Precision.HIGHEST

def matmul(left, right):
    return jnp.dot(left, right, precision=PRECISE, preferred_element_type=jnp.float32)

def layer_norm(values, gain):
    average = lax.optimization_barrier(jnp.mean(values, axis=-1, keepdims=True))
    centered = values - average
    variance = lax.optimization_barrier(jnp.mean(centered * centered, axis=-1, keepdims=True))
    return centered * lax.rsqrt(variance + EPS_NORM) * gain

def attend_sequence(queries, keys, values, prefix, valid):
    row_count = min(512, SEQ)
    block_total = SEQ // row_count
    starts = jnp.arange(block_total, dtype=jnp.int32) * row_count
    blocks = queries.reshape(block_total, row_count, HEADS, HEAD_DIM)
    score_scale = HEAD_DIM ** (-0.5)

    def one_block(inputs):
        query_rows, block_start = inputs
        rows_at = block_start + jnp.arange(row_count, dtype=jnp.int32)
        cols_at = jnp.arange(SEQ, dtype=jnp.int32)
        allowed = (cols_at[None, :] < valid) & ((cols_at[None, :] <= rows_at[:, None]) | (cols_at[None, :] < prefix))
        scores = jnp.einsum('qhd,khd->hqk', query_rows, keys, precision=PRECISE) * score_scale
        scores = low_back(scores)
        scores = jnp.where(allowed[None], scores, NEG_FILL)
        largest = lax.optimization_barrier(jnp.max(scores, axis=-1, keepdims=True))
        exponent = jnp.exp(scores - largest)
        soft_probs = exponent / lax.optimization_barrier(jnp.sum(exponent, axis=-1, keepdims=True))
        return jnp.einsum('hqk,khd->qhd', low(soft_probs), values, precision=PRECISE)
    mixed = lax.map(jax.checkpoint(one_block), (blocks, starts))
    return mixed.reshape(SEQ, HEADS, HEAD_DIM)

def one_layer(stream, prefix_group, valid_group, w_qkv, w_proj, w_up, w_down, gain_pair):
    group_seqs = prefix_group.shape[0]
    attn_in = low(layer_norm(stream, gain_pair[0]))
    qkv_rows = low(low_back(matmul(attn_in, w_qkv)))
    split = qkv_rows.reshape(group_seqs, SEQ, 3, HEADS, HEAD_DIM)
    mixed = jax.vmap(attend_sequence)(split[:, :, 0], split[:, :, 1], split[:, :, 2], prefix_group, valid_group)
    mixed = low(low_back(mixed.reshape(group_seqs * SEQ, D)))
    middle = stream + low_back(matmul(mixed, w_proj))
    ffn_in = low(layer_norm(middle, gain_pair[1]))
    hidden_pre = low_back(matmul(ffn_in, w_up))
    hidden = low(jax.nn.gelu(hidden_pre, approximate=False))
    return middle + low_back(matmul(hidden, w_down))

def adam_step(weight, first_moment, second, gradient, step_rate, weight_decay):
    first_new = BETA_ONE * first_moment + (1.0 - BETA_ONE) * gradient
    second_new = BETA_TWO * second + (1.0 - BETA_TWO) * gradient * gradient
    first_fix = 1.0 - BETA_ONE ** STEP_COUNT
    second_fix = 1.0 - BETA_TWO ** STEP_COUNT
    update = first_new / first_fix / (jnp.sqrt(second_new / second_fix) + EPS_ADAM)
    return (first_new, second_new, weight - step_rate * (update + weight_decay * weight))

def add_up(left, right):
    return left + right

def reference(tokens, cotangent, prefix_len, valid_len, qkv_weight, qkv_first, qkv_second, proj_weight, proj_first, proj_second, up_weight, up_first, up_second, down_weight, down_first, down_second, norm_gains, gains_first, gains_second):
    params = (qkv_weight, proj_weight, up_weight, down_weight, norm_gains)
    group = math.gcd(SEQS, max(1, 4096 // SEQ))
    group_total = SEQS // group
    tok_groups = tokens.reshape(group_total, group * SEQ, D)
    cot_groups = cotangent.reshape(group_total, group * SEQ, D)
    prefix_groups = prefix_len.reshape(group_total, group)
    valid_groups = valid_len.reshape(group_total, group)

    def run_group(carry, inputs):
        tok_group, cot_group, prefix_group, valid_group = inputs

        def forward(stream, weights):
            rounded = tuple((low(member) for member in weights))
            for layer_index in range(LAYERS):
                stream = one_layer(stream, prefix_group, valid_group, rounded[0][layer_index], rounded[1][layer_index], rounded[2][layer_index], rounded[3][layer_index], rounded[4][layer_index])
            return stream
        result, pullback = jax.vjp(forward, tok_group.astype(jnp.float32), params)
        positions = jnp.arange(SEQ, dtype=jnp.int32)
        live = (positions[None, :] < valid_group[:, None]).reshape(group * SEQ, 1)
        grad_in, grad_weights = pullback(jnp.where(live, cot_group.astype(jnp.float32), jnp.float32(0.0)))
        carry = jax.tree.map(add_up, carry, grad_weights)
        return (carry, (result.astype(jnp.bfloat16), grad_in.astype(jnp.bfloat16)))
    zero_grads = tuple((jnp.zeros(member.shape, jnp.float32) for member in params))
    grads, outputs = lax.scan(run_group, zero_grads, (tok_groups, cot_groups, prefix_groups, valid_groups))
    block_out = outputs[0].reshape(TOKENS, D)
    tokens_grad = outputs[1].reshape(TOKENS, D)
    rates = (2.5 / math.sqrt(D), 2.5 / math.sqrt(max(4 * D // SEQ, 1)), 2.5 / math.sqrt(D), 2.5 / math.sqrt(FF), 0.5)
    decays = (0.1, 0.1, 0.1, 0.1, 0.0)
    firsts = (qkv_first, proj_first, up_first, down_first, gains_first)
    seconds = (qkv_second, proj_second, up_second, down_second, gains_second)
    results = []
    for kind in range(5):
        results.extend(adam_step(params[kind], firsts[kind], seconds[kind], grads[kind], rates[kind], decays[kind]))
    return (block_out, tokens_grad, results[0], results[1], results[2], results[3], results[4], results[5], results[6], results[7], results[8], results[9], results[10], results[11], results[12], results[13], results[14])
```

```python
import functools
import math

import jax
import jax.numpy as jnp
from jax import lax
from jax.experimental import pallas as pl
from jax.experimental.pallas import tpu as pltpu
from jax.sharding import PartitionSpec as P

D = 384
HEADS = 6
HEAD_DIM = 64
FF = 1536
SEQ = 1024
STEP_COUNT = 7

NEG_FILL = -1e30
EPS_NORM = 1e-05
EPS_ADAM = 1e-08
BETA_ONE = 0.9
BETA_TWO = 0.99

LAYERS = 2
GROUPS = 4
CORES = 2
UNITS = GROUPS * CORES
BLOCK = 256
CHUNK = 512
QP, UP, DOWN = 0, 1, 2

MESH = pl.DeviceIdType.MESH
bf16 = jnp.bfloat16
f32 = jnp.float32


def dot(left, right, left_dim, right_dim):
    return lax.dot_general(
        left, right, (((left_dim,), (right_dim,)), ((), ())), preferred_element_type=f32
    )


def loop(count, body, unroll=1):
    def step(index, carry):
        body(index)
        return carry

    lax.fori_loop(0, count, step, 0, unroll=unroll)


class Remote:
    def __init__(self, src, dst, send, recv, device):
        self.made = lambda: pltpu.make_async_remote_copy(
            src_ref=src, dst_ref=dst, send_sem=send, recv_sem=recv,
            device_id=device, device_id_type=MESH,
        )

    def start(self):
        self.made().start()

    def wait_send(self):
        self.made().wait_send()

    def wait_recv(self):
        self.made().wait_recv()

    def wait(self):
        self.made().wait()


class Step:
    def __init__(self, sizes, refs):
        self.__dict__.update(sizes)
        self.__dict__.update(refs)
        self.dp = lax.axis_index("dp")
        self.z = lax.axis_index("fsdp")
        self.unit = self.dp % UNITS
        self.c = self.unit % CORES
        self.g = self.unit // CORES
        self.base = self.dp - self.unit
        self.core_peer = (self.base + self.g * CORES + (1 - self.c), self.z)
        gx, gy = self.g % 2, self.g // 2
        self.others = [gy * 2 + (1 - gx), (1 - gy) * 2 + gx, (1 - gy) * 2 + (1 - gx)]
        self.group_peers = [(self.base + g * CORES + self.c, self.z) for g in self.others]
        self.z_to = [(self.z + k) % self.Z for k in range(1, self.Z)]
        self.z_from = [(self.z + self.Z - k) % self.Z for k in range(1, self.Z)]
        self.z_peers = [(self.dp, z) for z in self.z_to]
        total = self.R * UNITS
        self.r_peers = [((self.dp + j * UNITS) % total, self.z) for j in range(1, self.R)]
        self.foreign = []
        size = 1
        while size < self.Z:
            at = self.z // size
            self.foreign.append(((at + 1 - 2 * (at % 2)) * size, size))
            size *= 2


    def remote(self, src, dst, send, recv, device):
        return Remote(src, dst, send, recv, device)

    def weight_unit(self, kind, layer, z, g, c):
        if kind == DOWN:
            return self.wdn.at[layer, z, g, c]
        whole = self.wqp if kind == QP else self.wup
        return whole.at[layer, z, c, :, pl.ds(pl.multiple_of(g * D, 128), D)]

    def weight_half(self, kind, layer, c):
        if kind == DOWN:
            return self.wdn.at[layer, :, :, c]
        return (self.wqp if kind == QP else self.wup).at[layer, :, c]

    def gather_z(self, m):
        layer, kind = divmod(m, 3)
        unit = lambda z: self.weight_unit(kind, layer, z, self.g, self.c)
        out = [
            self.remote(unit(self.z), unit(self.z), self.zs.at[m, k], self.zr.at[m, k], peer)
            for k, peer in enumerate(self.z_peers)
        ]
        into = [
            self.remote(unit(z), unit(z), self.zs.at[m, k], self.zr.at[m, k], self.z_peers[k])
            for k, z in enumerate(self.z_from)
        ]
        return out, into

    def gather_g(self, m):
        layer, kind = divmod(m, 3)
        out, into = [], []
        for k, peer in enumerate(self.group_peers):
            for b, (start, size) in enumerate(self.foreign):
                block = pl.ds(start, size)
                mine = self.weight_unit(kind, layer, block, self.g, self.c)
                theirs = self.weight_unit(kind, layer, block, self.others[k], self.c)
                i = k * len(self.foreign) + b
                out.append(self.remote(mine, mine, self.gs.at[m, i], self.gr.at[m, i], peer))
                into.append(self.remote(theirs, theirs, self.gs.at[m, i], self.gr.at[m, i], peer))
        return out, into

    def gather_c(self, m):
        layer, kind = divmod(m, 3)
        mine = self.weight_half(kind, layer, self.c)
        theirs = self.weight_half(kind, layer, 1 - self.c)
        out = self.remote(mine, mine, self.cs.at[m], self.cr.at[m], self.core_peer)
        into = self.remote(theirs, theirs, self.cs.at[m], self.cr.at[m], self.core_peer)
        return [out], [into]

    def start_z(self, m):
        for copy in self.gather_z(m)[0]:
            copy.start()

    def start_g(self, m):
        for copy in self.gather_z(m)[1]:
            copy.wait_recv()
        for copy in self.gather_g(m)[0]:
            copy.start()

    def start_c(self, m):
        for copy in self.gather_g(m)[1]:
            copy.wait_recv()
        for copy in self.gather_c(m)[0]:
            copy.start()

    def ready(self, m):
        for copy in self.gather_c(m)[1]:
            copy.wait_recv()

    def gather_sent(self):
        for m in range(3 * LAYERS):
            for copy in self.gather_z(m)[0] + self.gather_g(m)[0] + self.gather_c(m)[0]:
                copy.wait_send()


    def reduce_a(self, t):
        return self.remote(
            self.gb.at[t, :, :, 1 - self.c], self.ra.at[t],
            self.rs.at[t, 0], self.rr.at[t, 0], self.core_peer,
        )

    def reduce_b(self, t):
        return [
            self.remote(
                self.gb.at[t, self.others[k], :, self.c], self.rb.at[t, k],
                self.rs.at[t, 1 + k], self.rr.at[t, 1 + k], peer,
            )
            for k, peer in enumerate(self.group_peers)
        ]

    def reduce_c(self, m):
        layer, t = divmod(m, 3)
        return [
            self.remote(
                self.sc.at[t, self.z_to[k]], self.rc.at[layer, t, k],
                self.rs.at[t, 4 + k], self.rr.at[t, 4 + k], peer,
            )
            for k, peer in enumerate(self.z_peers)
        ]

    def reduce_r(self, m):
        layer, t = divmod(m, 3)
        return [
            self.remote(
                self.rx_out.at[layer, t], self.rx.at[layer, t, j],
                self.rxs.at[m, j], self.rxr.at[m, j], peer,
            )
            for j, peer in enumerate(self.r_peers)
        ]

    def reduce_d(self, m):
        layer, t = divmod(m, 3)
        at = 3 + self.Z
        mine = self.fin.at[layer, t, self.g, self.c]
        out, into = [], []
        for k, peer in enumerate(self.group_peers):
            theirs = self.fin.at[layer, t, self.others[k], self.c]
            sems = self.rs.at[t, at + k], self.rr.at[t, at + k]
            out.append(self.remote(mine, mine, *sems, peer))
            into.append(self.remote(theirs, theirs, *sems, peer))
        return out, into

    def reduce_e(self, m):
        layer, t = divmod(m, 3)
        sems = self.rs.at[t, 6 + self.Z], self.rr.at[t, 6 + self.Z]
        mine = self.fin.at[layer, t, :, self.c]
        theirs = self.fin.at[layer, t, :, 1 - self.c]
        return self.remote(mine, mine, *sems, self.core_peer), self.remote(
            theirs, theirs, *sems, self.core_peer
        )

    def grads_a(self, m):
        self.reduce_a(m % 3).start()

    def grads_b(self, m):
        t = m % 3
        copy = self.reduce_a(t)
        copy.wait()

        def add(g):
            both = self.gb[t, g, :, self.c].astype(f32) + self.ra[t, g].astype(f32)
            self.gb[t, g, :, self.c] = both.astype(bf16)

        loop(GROUPS, add)
        for copy in self.reduce_b(t):
            copy.start()

    def grads_c(self, m):
        t = m % 3
        for copy in self.reduce_b(t):
            copy.wait()
        total = self.gb[t, self.g, :, self.c].astype(f32)
        for k in range(GROUPS - 1):
            total = total + self.rb[t, k].astype(f32)
        self.sc[t] = total.astype(bf16)
        for copy in self.reduce_c(m):
            copy.start()

    def grads_d(self, m):
        layer, t = divmod(m, 3)
        for copy in self.reduce_c(m):
            copy.wait()
        total = self.sc[t, self.z].astype(f32)
        for k in range(self.Z - 1):
            total = total + self.rc[layer, t, k].astype(f32)
        if self.R > 1:
            self.rx_out[layer, t] = total.astype(bf16)
            for copy in self.reduce_r(m):
                copy.start()
            for copy in self.reduce_r(m):
                copy.wait()
            for j in range(self.R - 1):
                total = total + self.rx[layer, t, j].astype(f32)
        self.fin[layer, t, self.g, self.c] = total.astype(bf16)
        for copy in self.reduce_d(m)[0]:
            copy.start()

    def grads_e(self, m):
        out, into = self.reduce_d(m)
        for copy in into:
            copy.wait_recv()
        for copy in out:
            copy.wait_send()
        self.reduce_e(m)[0].start()

    def grads_f(self, m):
        layer, t = divmod(m, 3)
        out, into = self.reduce_e(m)
        into.wait_recv()
        out.wait_send()
        self.store(m).start()

    def store(self, m):
        layer, t = divmod(m, 3)
        return pltpu.make_async_copy(
            self.fin.at[layer, t], self.grads_out.at[layer, t], self.out_sem.at[2 + m]
        )


    def chunks(self, body, unroll=1):
        loop(self.T // CHUNK, lambda i: body(pl.ds(pl.multiple_of(i * CHUNK, CHUNK), CHUNK)), unroll)

    def spread(self, index):
        column = self.gcol[index]
        return jnp.concatenate([column] * (CHUNK // 128), axis=1)

    def normed(self, x, slot, at):
        mean = jnp.sum(x, axis=0, keepdims=True) * (1.0 / D)
        centered = x - mean
        inverse = lax.rsqrt(
            jnp.sum(centered * centered, axis=0, keepdims=True) * (1.0 / D) + EPS_NORM
        )
        self.stats[2 * slot : 2 * slot + 1, at] = mean
        self.stats[2 * slot + 1 : 2 * slot + 2, at] = inverse
        return centered * inverse

    def norm_back(self, grad, slot, at):
        mean = self.stats[2 * slot : 2 * slot + 1, at]
        inverse = self.stats[2 * slot + 1 : 2 * slot + 2, at]
        normed = (self.xs[slot, :, at] - mean) * inverse
        product = grad * normed
        partial = product[:, 0:128]
        for j in range(1, CHUNK // 128):
            partial = partial + product[:, j * 128 : (j + 1) * 128]
        self.gacc[slot] += partial
        gain = self.spread(slot)
        scaled = grad * gain
        average = jnp.sum(scaled, axis=0, keepdims=True) * (1.0 / D)
        along = jnp.sum(product * gain, axis=0, keepdims=True) * (1.0 / D)
        return inverse * (scaled - average - normed * along)

    def w_qkv(self, layer):
        return self.wqp[layer, :, :, :, 0 : 3 * D].reshape(D, 3 * D)

    def w_proj(self, layer):
        return self.wqp[layer, :, :, :, 3 * D : 4 * D].reshape(D, D)

    def w_up(self, layer):
        return self.wup[layer].reshape(D, FF)

    def w_down(self, layer):
        return self.wdn[layer].reshape(FF, D)

    def make_bias(self):
        prefix, valid = self.prefix[0], self.valid[0]
        key = lax.broadcasted_iota(jnp.int32, (BLOCK, BLOCK), 0)
        query = lax.broadcasted_iota(jnp.int32, (BLOCK, BLOCK), 1)
        causal = key <= query
        fill = lambda ok: jnp.where(ok, f32(0.0), f32(NEG_FILL))
        self.bias[0] = fill(causal | (key < prefix))
        self.bias[1] = fill(causal)
        self.bias[2] = fill(causal & (key + 2 * BLOCK < valid))
        self.bias[3] = fill(causal & (key + 3 * BLOCK < valid))
        self.bias[4] = fill(key + 2 * BLOCK < valid)

    def score_blocks(self, keys_t, queries, q):
        blocks = []
        for j in range(q + 1):
            s = dot(keys_t[j * BLOCK : (j + 1) * BLOCK], queries, 1, 0)
            if j == q:
                s = s + self.bias[q]
            elif j == 2:
                s = s + self.bias[4]
            blocks.append(s)
        return blocks

    def head_rows(self, h, part):
        return pl.ds(pl.multiple_of(part * D + h * HEAD_DIM, HEAD_DIM), HEAD_DIM)

    def attend(self, layer, h):
        queries = self.qkv[layer, self.head_rows(h, 0), :]
        keys_t = self.qkv[layer, self.head_rows(h, 1), :].T
        values = self.qkv[layer, self.head_rows(h, 2), :]
        values = jnp.concatenate([values, jnp.ones((16, self.T), bf16)], axis=0)
        for q in range(self.T // BLOCK):
            span = slice(q * BLOCK, (q + 1) * BLOCK)
            blocks = self.score_blocks(keys_t, queries[:, span], q)
            largest = functools.reduce(
                jnp.maximum, [jnp.max(s, axis=0, keepdims=True) for s in blocks]
            )
            probs = jnp.concatenate([jnp.exp(s - largest).astype(bf16) for s in blocks], axis=0)
            mixed = dot(values[:, : (q + 1) * BLOCK], probs, 1, 0)
            denominator = mixed[HEAD_DIM : HEAD_DIM + 1]
            mixed = mixed[:HEAD_DIM] * (1.0 / denominator)
            self.om[layer, self.head_rows(h, 0), span] = mixed.astype(bf16)
            self.lse[layer, h, :, span] = jnp.broadcast_to(
                largest + jnp.log(denominator), (8, BLOCK)
            )

    def attend_back(self, layer, h):
        queries = self.qkv[layer, self.head_rows(h, 0), :]
        keys = self.qkv[layer, self.head_rows(h, 1), :]
        keys_t = keys.T
        values_t = self.qkv[layer, self.head_rows(h, 2), :].T
        grads = self.dmix[self.head_rows(h, 0), :]
        mixed = self.om[layer, self.head_rows(h, 0), :]
        delta = jnp.sum(grads.astype(f32) * mixed.astype(f32), axis=0, keepdims=True)
        count = self.T // BLOCK
        key_grads, value_grads = [None] * count, [None] * count
        for q in range(count):
            span = slice(q * BLOCK, (q + 1) * BLOCK)
            q_rows, g_rows = queries[:, span], grads[:, span]
            blocks = self.score_blocks(keys_t, q_rows, q)
            total = self.lse[layer, h, 0:1, span]
            small = []
            for j, s in enumerate(blocks):
                probs = jnp.exp(s - total)
                slope = dot(values_t[j * BLOCK : (j + 1) * BLOCK], g_rows, 1, 0)
                low = probs.astype(bf16)
                d_scores = (probs * (slope - delta[:, span])).astype(bf16)
                small.append(d_scores)
                k_part = dot(q_rows, d_scores, 1, 1)
                v_part = dot(g_rows, low, 1, 1)
                key_grads[j] = k_part if key_grads[j] is None else key_grads[j] + k_part
                value_grads[j] = v_part if value_grads[j] is None else value_grads[j] + v_part
            d_all = jnp.concatenate(small, axis=0)
            q_part = dot(keys[:, : (q + 1) * BLOCK], d_all, 1, 0) * (HEAD_DIM**-0.5)
            self.dqkv[self.head_rows(h, 0), span] = q_part.astype(bf16)
        self.dqkv[self.head_rows(h, 1), :] = jnp.concatenate(key_grads, axis=1).astype(bf16)
        self.dqkv[self.head_rows(h, 2), :] = jnp.concatenate(value_grads, axis=1).astype(bf16)

    def first_norm(self, layer):
        slot = 2 * layer

        def body(at):
            n = self.normed(self.xs[slot, :, at], slot, at)
            self.an[layer, :, at] = (n * self.spread(slot)).astype(bf16)

        self.chunks(body)

    def project_in(self, layer):
        def body(at):
            rows = dot(self.w_qkv(layer), self.an[layer, :, at], 0, 0)
            self.qkv[layer, 0:D, at] = (rows[0:D] * (HEAD_DIM**-0.5)).astype(bf16)
            self.qkv[layer, D : 3 * D, at] = rows[D:].astype(bf16)

        self.chunks(body)

    def middle(self, layer):
        slot = 2 * layer + 1

        def body(at):
            x = self.xs[slot - 1, :, at] + dot(self.w_proj(layer), self.om[layer, :, at], 0, 0)
            self.xs[slot, :, at] = x
            n = self.normed(x, slot, at)
            self.bn[layer, :, at] = (n * self.spread(slot)).astype(bf16)

        self.chunks(body)

    def feed(self, layer):
        def body(at):
            u = dot(self.w_up(layer), self.bn[layer, :, at], 0, 0)
            area = 0.5 + 0.5 * lax.erf(u * (0.5**0.5))
            density = jnp.exp(u * u * (-0.5)) * (1.0 / math.sqrt(2.0 * math.pi))
            hidden = (u * area).astype(bf16)
            self.hid[layer, :, at] = hidden
            self.slope[layer, :, at] = (area + u * density).astype(bf16)
            x = self.xs[2 * layer + 1, :, at] + dot(self.w_down(layer), hidden, 0, 0)
            if layer + 1 < LAYERS:
                self.xs[2 * layer + 2, :, at] = x
            else:
                self.toks[at, :] = x.astype(bf16).T

        self.chunks(body)

    def feed_back(self, layer):
        slot = 2 * layer + 1

        def body(at):
            low = self.dy[:, at].astype(bf16)
            self.dm[:, at] = low
            d_hidden = dot(self.w_down(layer), low, 1, 0)
            d_pre = (d_hidden * self.slope[layer, :, at].astype(f32)).astype(bf16)
            self.slope[layer, :, at] = d_pre
            grad = dot(self.w_up(layer), d_pre, 1, 0)
            total = self.dy[:, at] + self.norm_back(grad, slot, at)
            self.dy[:, at] = total
            low = total.astype(bf16)
            self.datt[:, at] = low
            self.dmix[:, at] = dot(self.w_proj(layer), low, 1, 0).astype(bf16)

        self.chunks(body)

    def down_grad(self, layer):
        width = FF // self.Z

        def body(z):
            rows = self.hid[layer, pl.ds(pl.multiple_of(z * width, 64), width), :]
            value = dot(rows, self.dm[...], 1, 1).astype(bf16)
            self.gb[DOWN, :, z] = value.reshape(GROUPS, CORES, self.UR, D)

        loop(self.Z, body)

    def store_grad(self, t, g, value):
        self.gb[t, g] = value.astype(bf16).reshape(self.Z, CORES, self.UR, D)

    def up_grad(self, layer):
        def body(g):
            rows = self.slope[layer, pl.ds(pl.multiple_of(g * D, 64), D), :]
            self.store_grad(UP, g, dot(self.bn[layer], rows, 1, 1))

        loop(GROUPS, body)

    def proj_grad(self, layer):
        self.store_grad(QP, 3, dot(self.om[layer], self.datt[...], 1, 1))

    def qkv_grad(self, layer):
        def body(g):
            rows = self.dqkv[pl.ds(pl.multiple_of(g * D, 64), D), :]
            self.store_grad(QP, g, dot(self.an[layer], rows, 1, 1))

        loop(3, body)

    def qkv_back(self, layer):
        slot = 2 * layer

        def body(at):
            grad = dot(self.w_qkv(layer), self.dqkv[:, at], 1, 0)
            total = self.dy[:, at] + self.norm_back(grad, slot, at)
            self.dy[:, at] = total
            if layer == 0:
                self.cots[at, :] = total.astype(bf16).T

        self.chunks(body)


    def gain_slots(self):
        out, into = [], []
        for k, peer in enumerate(self.z_peers):
            mine, theirs = self.gslot.at[self.z], self.gslot.at[self.z_from[k]]
            out.append(self.remote(mine, mine, self.ns.at[k], self.nr.at[k], peer))
            into.append(self.remote(theirs, theirs, self.ns.at[k], self.nr.at[k], peer))
        return out, into

    def swap_gains(self, first, peers):
        copies = [
            self.remote(
                self.nsum.at[first], self.nin.at[first + k],
                self.ns.at[self.Z - 1 + first + k], self.nr.at[self.Z - 1 + first + k], peer,
            )
            for k, peer in enumerate(peers)
        ]
        return copies

    def fold_gains(self, first, peers, target):
        for copy in self.swap_gains(first, peers):
            copy.wait()
        total = self.nsum[first]
        for k in range(len(peers)):
            total = total + self.nin[first + k]
        self.nsum[target] = total


    def run(self):
        Z = self.Z
        loads = [
            pltpu.make_async_copy(src, dst, self.in_sem.at[i])
            for i, (src, dst) in enumerate(
                [(self.tokens, self.toks), (self.cotangent, self.cots)]
                + [
                    pair
                    for layer in range(LAYERS)
                    for pair in (
                        (self.qkv_w.at[layer, self.c], self.sq.at[layer]),
                        (self.proj_w.at[layer, self.c], self.sp.at[layer]),
                        (self.up_w.at[layer, self.c], self.su.at[layer]),
                        (self.down_w.at[layer, :, self.c], self.sd.at[layer]),
                    )
                ]
            )
        ]
        for i in (2, 3, 0, 4, 5, 6, 7, 8, 9, 1):
            loads[i].start()
        self.gslot[...] = jnp.zeros_like(self.gslot)
        for layer in range(LAYERS):
            rounded = self.gains[layer].astype(bf16).astype(f32)
            self.gslot[self.z, 2 * layer : 2 * layer + 2, 0 : D // Z] = rounded
        self.gacc[...] = jnp.zeros_like(self.gacc)

        barrier = pltpu.get_barrier_semaphore()
        peers = [self.core_peer] + self.group_peers + self.z_peers + self.r_peers
        for peer in peers:
            pl.semaphore_signal(barrier, inc=1, device_id=peer, device_id_type=MESH)
        pl.semaphore_wait(barrier, len(peers))

        for copy in self.gain_slots()[0]:
            copy.start()
        for layer in range(LAYERS):
            at = 2 + 4 * layer
            loads[at].wait()
            loads[at + 1].wait()
            self.wqp[layer, self.z, self.c, :, 0 : 3 * D] = self.sq[layer].astype(bf16)
            self.wqp[layer, self.z, self.c, :, 3 * D : 4 * D] = self.sp[layer].astype(bf16)
            self.start_z(3 * layer + QP)
            loads[at + 2].wait()
            self.wup[layer, self.z, self.c] = self.su[layer].astype(bf16)
            self.start_z(3 * layer + UP)
            loads[at + 3].wait()
            self.wdn[layer, self.z, :, self.c] = self.sd[layer].astype(bf16)
            self.start_z(3 * layer + DOWN)
        loads[0].wait()

        def take(at):
            self.xs[0, :, at] = self.toks[at, :].T.astype(f32)

        self.chunks(take)
        self.start_g(0)
        for copy in self.gain_slots()[1]:
            copy.wait_recv()
        for copy in self.gain_slots()[0]:
            copy.wait_send()
        for z in range(Z):
            tall = jnp.concatenate([self.gslot[z]] * 16, axis=0).T
            for i in range(2 * LAYERS):
                self.gcol[i, z * (D // Z) : (z + 1) * (D // Z), :] = jnp.broadcast_to(
                    tall[0 : D // Z, i : i + 1], (D // Z, 128)
                )
        self.make_bias()
        self.first_norm(0)
        self.start_g(1)
        self.start_c(0)
        self.start_g(2)
        self.ready(0)
        self.project_in(0)
        self.start_c(1)
        self.start_g(3)
        loop(HEADS, lambda h: self.attend(0, h))
        self.start_c(2)
        self.start_g(4)
        self.ready(1)
        self.middle(0)
        self.start_g(5)
        self.ready(2)
        self.feed(0)
        self.start_c(3)
        self.first_norm(1)
        self.ready(3)
        self.project_in(1)
        self.start_c(4)
        loop(HEADS, lambda h: self.attend(1, h))
        self.start_c(5)
        self.ready(4)
        self.middle(1)
        self.ready(5)
        self.feed(1)
        out_copy = pltpu.make_async_copy(self.toks, self.block_out, self.out_sem.at[0])
        out_copy.start()
        self.gather_sent()

        loads[1].wait()
        valid = self.valid[0]

        def start_back(at):
            where = at.start + lax.broadcasted_iota(jnp.int32, (D, CHUNK), 1)
            grad = self.cots[at, :].T.astype(f32)
            self.dy[:, at] = jnp.where(where < valid, grad, f32(0.0))

        self.chunks(start_back)

        self.feed_back(1)
        self.down_grad(1)
        self.grads_a(5)
        self.up_grad(1)
        self.grads_a(4)
        self.proj_grad(1)
        self.grads_b(5)

        def heads_one(h):
            self.attend_back(1, h)
            pl.when(h == 0)(lambda: self.grads_b(4))
            pl.when(h == 1)(lambda: self.grads_c(5))
            pl.when(h == 2)(lambda: self.grads_c(4))
            pl.when(h == 3)(lambda: self.grads_d(5))
            pl.when(h == 4)(lambda: self.grads_d(4))

        loop(HEADS, heads_one)
        self.grads_e(5)
        self.grads_e(4)
        self.qkv_grad(1)
        self.grads_a(3)
        self.qkv_back(1)

        self.feed_back(0)
        self.grads_b(3)
        self.down_grad(0)
        self.grads_f(5)
        self.grads_a(2)
        self.up_grad(0)
        self.grads_f(4)
        self.grads_a(1)
        self.grads_c(3)
        self.proj_grad(0)
        self.grads_b(2)

        def heads_zero(h):
            self.attend_back(0, h)
            pl.when(h == 0)(lambda: self.grads_d(3))
            pl.when(h == 1)(lambda: self.grads_b(1))
            pl.when(h == 2)(lambda: self.grads_c(2))
            pl.when(h == 2)(lambda: self.grads_e(3))
            pl.when(h == 3)(lambda: self.grads_c(1))
            pl.when(h == 4)(lambda: self.grads_d(2))

        loop(HEADS, heads_zero)
        self.grads_d(1)
        self.grads_f(3)
        self.qkv_grad(0)
        self.grads_a(0)
        self.grads_e(2)
        self.grads_e(1)
        self.qkv_back(0)
        grad_copy = pltpu.make_async_copy(self.cots, self.tokens_grad, self.out_sem.at[1])
        grad_copy.start()
        self.grads_b(0)

        lane = lax.broadcasted_iota(jnp.int32, (D, 128), 1)
        tall = jnp.zeros((D, 128), f32)
        for i in range(2 * LAYERS):
            column = jnp.sum(self.gacc[i], axis=1, keepdims=True)
            tall = tall + jnp.where(lane == i, column, f32(0.0))
        self.nsum[0] = tall.T[0:8]
        stages = [[self.core_peer], self.group_peers, self.z_peers]
        if self.R > 1:
            stages.append(self.r_peers)
        firsts = [0, 1, 1 + len(self.group_peers), 1 + len(self.group_peers) + Z - 1]
        last = firsts[len(stages) - 1] + len(stages[-1])
        ends = firsts[1 : len(stages)] + [last]
        for copy in self.swap_gains(0, stages[0]):
            copy.start()
        self.fold_gains(0, stages[0], ends[0])
        for copy in self.swap_gains(firsts[1], stages[1]):
            copy.start()
        self.grads_f(2)
        self.grads_f(1)
        self.grads_c(0)
        for i in range(1, len(stages)):
            self.fold_gains(firsts[i], stages[i], ends[i])
            if i + 1 < len(stages):
                for copy in self.swap_gains(firsts[i + 1], stages[i + 1]):
                    copy.start()
        self.grads_d(0)
        tall = jnp.concatenate([self.nsum[last]] * 16, axis=0).T
        self.gcol[0] = tall
        width = D // Z
        mine = self.gcol[0, pl.ds(pl.multiple_of(self.z * width, 8), width), :]
        mine = jnp.concatenate([mine, jnp.zeros((128 - width, 128), f32)], axis=0).T
        self.gains_grad[...] = mine[0:8]
        self.grads_e(0)
        self.grads_f(0)
        out_copy.wait()
        grad_copy.wait()
        for m in range(3 * LAYERS):
            self.store(m).wait()


def adam(weight, first, second, grad, rate, decay):
    first_new = BETA_ONE * first + (1.0 - BETA_ONE) * grad
    second_new = BETA_TWO * second + (1.0 - BETA_TWO) * grad * grad
    first_fix = 1.0 - BETA_ONE**STEP_COUNT
    second_fix = 1.0 - BETA_TWO**STEP_COUNT
    update = first_new / first_fix / (jnp.sqrt(second_new / second_fix) + EPS_ADAM)
    return first_new, second_new, weight - rate * (update + decay * weight)


def adam_kernel(*refs):
    (block_in, tgrad_in, grads, gains_grad) = refs[:4]
    masters = refs[4:19]
    block_out, tgrad_out = refs[19:21]
    outs = refs[21:]
    rates = (
        2.5 / math.sqrt(D),
        2.5 / math.sqrt(max(4 * D // SEQ, 1)),
        2.5 / math.sqrt(D),
        2.5 / math.sqrt(FF),
        0.5,
    )
    block_out[...] = block_in[...]
    tgrad_out[...] = tgrad_in[...]

    def update(kind, index, grad):
        weight, first, second = (masters[3 * kind + j] for j in range(3))
        new = adam(
            weight[index], first[index], second[index], grad, rates[kind],
            0.1 if kind < 4 else 0.0,
        )
        for j in range(3):
            outs[3 * kind + j][index] = new[j]

    for g in range(GROUPS):
        grad = grads[0, QP, g, 0].astype(f32)
        if g < 3:
            update(0, (0, 0, slice(None), slice(g * D, (g + 1) * D)), grad)
        else:
            update(1, (0, 0), grad)
        update(2, (0, 0, slice(None), slice(g * D, (g + 1) * D)), grads[0, UP, g, 0].astype(f32))
        update(3, (0, g, 0), grads[0, DOWN, g, 0].astype(f32))
    width = masters[12].shape[-1]
    for layer in range(LAYERS):
        update(4, (layer,), gains_grad[2 * layer : 2 * layer + 2, 0:width])


def make_per_device(n_dp, n_fsdp):
    Z, R = n_fsdp, n_dp // UNITS
    UR = D // Z // CORES

    def per_device(
        tokens, cotangent, prefix_len, valid_len,
        qkv_weight, qkv_first, qkv_second,
        proj_weight, proj_first, proj_second,
        up_weight, up_first, up_second,
        down_weight, down_first, down_second,
        norm_gains, gains_first, gains_second,
    ):
        T = tokens.shape[0]
        assert prefix_len.shape == (1,) and T == 4 * BLOCK
        assert FF // Z // UNITS == UR
        rows4 = lambda w: w.reshape(LAYERS, CORES, UR, w.shape[-1])
        rows5 = lambda w: w.reshape(LAYERS, GROUPS, CORES, UR, D)
        vmem = pltpu.VMEM
        scratch = dict(
            wqp=vmem((LAYERS, Z, CORES, UR, 4 * D), bf16),
            wup=vmem((LAYERS, Z, CORES, UR, FF), bf16),
            wdn=vmem((LAYERS, Z, GROUPS, CORES, UR, D), bf16),
            sq=vmem((LAYERS, UR, 3 * D), f32),
            sp=vmem((LAYERS, UR, D), f32),
            su=vmem((LAYERS, UR, FF), f32),
            sd=vmem((LAYERS, GROUPS, UR, D), f32),
            gslot=vmem((Z, 8, 128), f32),
            gcol=vmem((2 * LAYERS, D, 128), f32),
            gacc=vmem((2 * LAYERS, D, 128), f32),
            xs=vmem((2 * LAYERS, D, T), f32),
            dy=vmem((D, T), f32),
            an=vmem((LAYERS, D, T), bf16),
            bn=vmem((LAYERS, D, T), bf16),
            qkv=vmem((LAYERS, 3 * D, T), bf16),
            om=vmem((LAYERS, D, T), bf16),
            hid=vmem((LAYERS, FF, T), bf16),
            slope=vmem((LAYERS, FF, T), bf16),
            dqkv=vmem((3 * D, T), bf16),
            dmix=vmem((D, T), bf16),
            dm=vmem((D, T), bf16),
            datt=vmem((D, T), bf16),
            lse=vmem((LAYERS, HEADS, 8, T), f32),
            stats=vmem((4 * LAYERS, T), f32),
            bias=vmem((5, BLOCK, BLOCK), f32),
            toks=vmem((T, D), bf16),
            cots=vmem((T, D), bf16),
            gb=vmem((3, GROUPS, Z, CORES, UR, D), bf16),
            ra=vmem((3, GROUPS, Z, UR, D), bf16),
            rb=vmem((3, GROUPS - 1, Z, UR, D), bf16),
            sc=vmem((3, Z, UR, D), bf16),
            rc=vmem((LAYERS, 3, Z - 1, UR, D), bf16),
            fin=vmem((LAYERS, 3, GROUPS, CORES, UR, D), bf16),
            nsum=vmem((8 + Z + R, 8, D), f32),
            nin=vmem((8 + Z + R, 8, D), f32),
        )
        sem = pltpu.SemaphoreType.DMA
        levels = Z.bit_length() - 1
        scratch.update(
            zs=sem((3 * LAYERS, Z - 1)),
            zr=sem((3 * LAYERS, Z - 1)),
            gs=sem((3 * LAYERS, 3 * levels)),
            gr=sem((3 * LAYERS, 3 * levels)),
            cs=sem((3 * LAYERS,)),
            cr=sem((3 * LAYERS,)),
            rs=sem((3, 7 + Z)),
            rr=sem((3, 7 + Z)),
            ns=sem((2 * Z + R + 4,)),
            nr=sem((2 * Z + R + 4,)),
            in_sem=sem((2 + 4 * LAYERS,)),
            out_sem=sem((2 + 3 * LAYERS,)),
        )
        if R > 1:
            scratch.update(
                rx=vmem((LAYERS, 3, R - 1, UR, D), bf16),
                rx_out=vmem((LAYERS, 3, UR, D), bf16),
                rxs=sem((3 * LAYERS, R - 1)),
                rxr=sem((3 * LAYERS, R - 1)),
            )
        ins = dict(
            tokens=tokens, cotangent=cotangent, prefix=prefix_len, valid=valid_len,
            qkv_w=rows4(qkv_weight), proj_w=rows4(proj_weight), up_w=rows4(up_weight),
            down_w=rows5(down_weight), gains=norm_gains,
        )
        outs = dict(
            block_out=jax.ShapeDtypeStruct((T, D), bf16),
            tokens_grad=jax.ShapeDtypeStruct((T, D), bf16),
            grads_out=jax.ShapeDtypeStruct((LAYERS, 3, GROUPS, CORES, UR, D), bf16),
            gains_grad=jax.ShapeDtypeStruct((8, 128), f32),
        )
        names = list(ins) + list(outs) + list(scratch)
        hbm = pl.BlockSpec(memory_space=pl.ANY)
        smem = pl.BlockSpec(memory_space=pltpu.SMEM)
        local = pl.BlockSpec(memory_space=pltpu.VMEM)

        def kernel(*refs):
            Step(dict(T=T, Z=Z, R=R, UR=UR), dict(zip(names, refs))).run()

        block_mid, tgrad_mid, grads, gains_grad = pl.pallas_call(
            kernel,
            out_shape=list(outs.values()),
            in_specs=[hbm, hbm, smem, smem, hbm, hbm, hbm, hbm, local],
            out_specs=[hbm, hbm, hbm, local],
            scratch_shapes=list(scratch.values()),
            compiler_params=pltpu.CompilerParams(
                collective_id=0, has_side_effects=True, vmem_limit_bytes=62 * 1024 * 1024
            ),
            name="train_step",
        )(*ins.values())

        masters = [
            f(w)
            for f, group in (
                (rows4, (qkv_weight, qkv_first, qkv_second)),
                (rows4, (proj_weight, proj_first, proj_second)),
                (rows4, (up_weight, up_first, up_second)),
                (rows5, (down_weight, down_first, down_second)),
                (lambda w: w, (norm_gains, gains_first, gains_second)),
            )
            for w in group
        ]
        tok_block = pl.BlockSpec((T // 4, D), lambda l, c: (2 * l + c, 0))

        def spec(w):
            if w.ndim == 4:
                return pl.BlockSpec((1, 1, *w.shape[2:]), lambda l, c: (l, c, 0, 0))
            if w.ndim == 5:
                return pl.BlockSpec((1, GROUPS, 1, UR, D), lambda l, c: (l, 0, c, 0, 0))
            return pl.BlockSpec(w.shape, lambda l, c: (0, 0, 0))

        specs = [spec(w) for w in masters]
        done = pl.pallas_call(
            adam_kernel,
            grid=(LAYERS, CORES),
            out_shape=[jax.ShapeDtypeStruct((T, D), bf16)] * 2
            + [jax.ShapeDtypeStruct(w.shape, f32) for w in masters],
            in_specs=[
                tok_block,
                tok_block,
                pl.BlockSpec((1, 3, GROUPS, 1, UR, D), lambda l, c: (l, 0, 0, c, 0, 0)),
                pl.BlockSpec((8, 128), lambda l, c: (0, 0)),
                *specs,
            ],
            out_specs=[tok_block, tok_block, *specs],
            compiler_params=pltpu.CompilerParams(vmem_limit_bytes=48 * 1024 * 1024),
            name="adam",
        )(block_mid, tgrad_mid, grads, gains_grad, *masters)
        shapes = [
            w.shape
            for w in (
                qkv_weight, qkv_first, qkv_second, proj_weight, proj_first, proj_second,
                up_weight, up_first, up_second, down_weight, down_first, down_second,
                norm_gains, gains_first, gains_second,
            )
        ]
        news = [x.reshape(s) for x, s in zip(done[2:], shapes)]
        results = []
        for kind in range(5):
            weight_new, second_new, first_new = news[3 * kind + 2], news[3 * kind + 1], news[3 * kind]
            results += [first_new, second_new, weight_new]
        return (done[0], done[1], *results)

    return per_device


def solution(mesh):
    rows = P(("dp", "fsdp"), None)
    lens = P(("dp", "fsdp"))
    weight = P(None, "fsdp", None)
    gain = P(None, None, "fsdp")
    return jax.shard_map(
        make_per_device(mesh.shape["dp"], mesh.shape["fsdp"]),
        mesh=mesh,
        in_specs=(rows, rows, lens, lens, *([weight] * 12), *([gain] * 3)),
        out_specs=(rows, rows, *([weight] * 12), *([gain] * 3)),
        check_vma=False,
    )
```

```python
import functools
import math

import jax
import jax.numpy as jnp
from jax import lax
from jax.experimental import pallas as pl
from jax.experimental.pallas import tpu as pltpu
from jax.sharding import PartitionSpec as P

D = 384
HEADS = 6
HEAD_DIM = 64
FF = 1536
SEQ = 1024
STEP_COUNT = 7

NEG_FILL = -1e30
EPS_NORM = 1e-05
EPS_ADAM = 1e-08
BETA_ONE = 0.9
BETA_TWO = 0.99

LAYERS = 2
GROUPS = 4
CORES = 2
UNITS = GROUPS * CORES
BLOCK = 256
CHUNK = 512
QP, UP, DOWN = 0, 1, 2
PAIR = 2 * HEAD_DIM
ITEMS = [(layer, kind, kind, pl.ds(0, D)) for layer, kind in ((1, DOWN), (1, UP), (1, QP), (0, DOWN), (0, UP))]
ITEMS += [(0, QP, 3, pl.ds(p * PAIR, PAIR)) for p in range(3)]
D1, U1, Q1, D0, U0, P0, P1, P2 = range(8)
LAST = P2

MESH = pl.DeviceIdType.MESH
bf16 = jnp.bfloat16
f32 = jnp.float32


def dot(left, right, left_dim, right_dim):
    return lax.dot_general(
        left, right, (((left_dim,), (right_dim,)), ((), ())), preferred_element_type=f32
    )


def loop(count, body, unroll=1):
    def step(index, carry):
        body(index)
        return carry

    lax.fori_loop(0, count, step, 0, unroll=unroll)


class Remote:
    def __init__(self, src, dst, send, recv, device):
        self.made = lambda: pltpu.make_async_remote_copy(
            src_ref=src, dst_ref=dst, send_sem=send, recv_sem=recv,
            device_id=device, device_id_type=MESH,
        )

    def start(self):
        self.made().start()

    def wait_send(self):
        self.made().wait_send()

    def wait_recv(self):
        self.made().wait_recv()

    def wait(self):
        self.made().wait()


class Step:
    def __init__(self, sizes, refs):
        self.__dict__.update(sizes)
        self.__dict__.update(refs)
        self.dp = lax.axis_index("dp")
        self.z = lax.axis_index("fsdp")
        self.unit = self.dp % UNITS
        self.c = self.unit % CORES
        self.g = self.unit // CORES
        self.base = self.dp - self.unit
        self.core_peer = (self.base + self.g * CORES + (1 - self.c), self.z)
        gx, gy = self.g % 2, self.g // 2
        self.gx, self.gy = gx, gy
        self.others = [gy * 2 + (1 - gx), (1 - gy) * 2 + gx, (1 - gy) * 2 + (1 - gx)]
        self.group_peers = [(self.base + g * CORES + self.c, self.z) for g in self.others]
        self.z_others = []
        for k in range(1, self.Z):
            other, bit = 0, 1
            while bit < self.Z:
                own = (self.z // bit) % 2
                other = other + bit * (1 - own if k & bit else own)
                bit *= 2
            self.z_others.append(other)
        self.z_peers = [(self.dp, z) for z in self.z_others]
        total = self.R * UNITS
        self.r_peers = [((self.dp + j * UNITS) % total, self.z) for j in range(1, self.R)]


    def remote(self, src, dst, send, recv, device):
        return Remote(src, dst, send, recv, device)

    def weight_unit(self, kind, layer, z, g, c):
        if kind == DOWN:
            return self.wdn.at[layer, z, g, c]
        whole = self.wqp if kind == QP else self.wup
        return whole.at[layer, z, c, :, pl.ds(pl.multiple_of(g * D, 128), D)]

    def weight_half(self, kind, layer, z, c):
        if kind == DOWN:
            return self.wdn.at[layer, z, :, c]
        return (self.wqp if kind == QP else self.wup).at[layer, z, c]

    def gather_z(self, m):
        layer, kind = divmod(m, 3)
        unit = lambda z: self.weight_unit(kind, layer, z, self.g, self.c)
        out, into = [], []
        for k, peer in enumerate(self.z_peers):
            sems = self.zs.at[m, k], self.zr.at[m, k]
            out.append(self.remote(unit(self.z), unit(self.z), *sems, peer))
            into.append(self.remote(unit(self.z_others[k]), unit(self.z_others[k]), *sems, peer))
        return out, into

    def gather_g(self, m, k):
        layer, kind = divmod(m, 3)
        unit = lambda g: self.weight_unit(kind, layer, self.z_others[k], g, self.c)
        out, into = [], []
        for j, peer in enumerate(self.group_peers):
            sems = self.gs.at[m, 3 * k + j], self.gr.at[m, 3 * k + j]
            out.append(self.remote(unit(self.g), unit(self.g), *sems, peer))
            into.append(self.remote(unit(self.others[j]), unit(self.others[j]), *sems, peer))
        return out, into

    def gather_c(self, m, k):
        layer, kind = divmod(m, 3)
        z = self.z if k == self.Z - 1 else self.z_others[k]
        half = lambda c: self.weight_half(kind, layer, z, c)
        sems = self.cs.at[m, k], self.cr.at[m, k]
        out = self.remote(half(self.c), half(self.c), *sems, self.core_peer)
        into = self.remote(half(1 - self.c), half(1 - self.c), *sems, self.core_peer)
        return out, into

    def start_z(self, m):
        for copy in self.gather_z(m)[0]:
            copy.start()
        self.gather_c(m, self.Z - 1)[0].start()

    def start_g(self, m):
        into = self.gather_z(m)[1]
        for k in range(self.Z - 1):
            into[k].wait_recv()
            for copy in self.gather_g(m, k)[0]:
                copy.start()

    def start_c(self, m):
        for k in range(self.Z - 1):
            for copy in self.gather_g(m, k)[1]:
                copy.wait_recv()
            self.gather_c(m, k)[0].start()

    def ready(self, m):
        for k in range(self.Z):
            self.gather_c(m, k)[1].wait_recv()

    def gather_sent(self):
        for m in range(3 * LAYERS):
            copies = self.gather_z(m)[0] + [self.gather_c(m, k)[0] for k in range(self.Z)]
            for k in range(self.Z - 1):
                copies += self.gather_g(m, k)[0]
            for copy in copies:
                copy.wait_send()


    def reduce_a(self, i):
        layer, t, buf, cols = ITEMS[i]
        return [
            self.remote(
                self.gb.at[t, :, :, :, 1 - self.c, :, cols], self.ra.at[buf, :, :, :, :, cols],
                self.rs.at[i, 0], self.rr.at[i, 0], self.core_peer,
            )
        ]

    def reduce_b1(self, i):
        layer, t, buf, cols = ITEMS[i]
        half = self.Z // 2
        return [
            self.remote(
                self.gb.at[t, :, 1 - self.gx, 0:half, self.c, :, cols],
                self.rb1.at[buf, 0, :, :, :, cols],
                self.rs.at[i, 1], self.rr.at[i, 1], self.group_peers[0],
            ),
            self.remote(
                self.gb.at[t, 1 - self.gy, :, half:, self.c, :, cols],
                self.rb1.at[buf, 1, :, :, :, cols],
                self.rs.at[i, 2], self.rr.at[i, 2], self.group_peers[1],
            ),
        ]

    def reduce_b2(self, i):
        layer, t, buf, cols = ITEMS[i]
        half = self.Z // 2
        return [
            self.remote(
                self.gb.at[t, 1 - self.gy, self.gx, 0:half, self.c, :, cols],
                self.rb2.at[buf, 0, :, :, cols],
                self.rs.at[i, 3], self.rr.at[i, 3], self.group_peers[1],
            ),
            self.remote(
                self.gb.at[t, self.gy, 1 - self.gx, half:, self.c, :, cols],
                self.rb2.at[buf, 1, :, :, cols],
                self.rs.at[i, 4], self.rr.at[i, 4], self.group_peers[0],
            ),
        ]

    def reduce_b(self, i):
        layer, t, buf, cols = ITEMS[i]
        return [
            self.remote(
                self.gb.at[t, self.others[k] // 2, self.others[k] % 2, :, self.c, :, cols],
                self.rb.at[k],
                self.rs.at[i, 1 + k], self.rr.at[i, 1 + k], peer,
            )
            for k, peer in enumerate(self.group_peers)
        ]

    def reduce_c(self, i):
        layer, t, buf, cols = ITEMS[i]
        return [
            self.remote(
                self.sc.at[buf, self.z_others[k], :, cols], self.rc.at[layer, t, k, :, cols],
                self.rs.at[i, 5 + k], self.rr.at[i, 5 + k], peer,
            )
            for k, peer in enumerate(self.z_peers)
        ]

    def reduce_r(self, i):
        layer, t, buf, cols = ITEMS[i]
        return [
            self.remote(
                self.rx_out.at[layer, t, :, cols], self.rx.at[layer, t, j, :, cols],
                self.rxs.at[i, j], self.rxr.at[i, j], peer,
            )
            for j, peer in enumerate(self.r_peers)
        ]

    def reduce_d(self, i):
        layer, t, buf, cols = ITEMS[i]
        at = 4 + self.Z
        mine = self.fin.at[layer, t, self.g, self.c, :, cols]
        out, into = [], []
        for k, peer in enumerate(self.group_peers):
            theirs = self.fin.at[layer, t, self.others[k], self.c, :, cols]
            sems = self.rs.at[i, at + k], self.rr.at[i, at + k]
            out.append(self.remote(mine, mine, *sems, peer))
            into.append(self.remote(theirs, theirs, *sems, peer))
        return out, into

    def reduce_e(self, i):
        layer, t, buf, cols = ITEMS[i]
        sems = self.rs.at[i, 7 + self.Z], self.rr.at[i, 7 + self.Z]
        mine = self.fin.at[layer, t, :, self.c, :, cols]
        theirs = self.fin.at[layer, t, :, 1 - self.c, :, cols]
        return [self.remote(mine, mine, *sems, self.core_peer)], [
            self.remote(theirs, theirs, *sems, self.core_peer)
        ]

    def each(self, copies, action):
        for copy in copies:
            getattr(copy, action)()

    def grads_a(self, i):
        self.each(self.reduce_a(i), "start")

    def add_cores(self, i):
        layer, t, buf, cols = ITEMS[i]
        self.each(self.reduce_a(i), "wait")

        def add(g):
            at = (t, g // 2, g % 2, slice(None), self.c, slice(None), cols)
            both = self.gb[at].astype(f32) + self.ra[buf, g // 2, g % 2, :, :, cols].astype(f32)
            self.gb[at] = both.astype(bf16)

        loop(GROUPS, add)

    def grads_b1(self, i):
        self.add_cores(i)
        self.each(self.reduce_b1(i), "start")

    def grads_b2(self, i):
        layer, t, buf, cols = ITEMS[i]
        half = self.Z // 2
        self.each(self.reduce_b1(i), "wait")
        at = (t, slice(None), self.gx, slice(0, half), self.c, slice(None), cols)
        both = self.gb[at].astype(f32) + self.rb1[buf, 0, :, :, :, cols].astype(f32)
        self.gb[at] = both.astype(bf16)
        at = (t, self.gy, slice(None), slice(half, self.Z), self.c, slice(None), cols)
        both = self.gb[at].astype(f32) + self.rb1[buf, 1, :, :, :, cols].astype(f32)
        self.gb[at] = both.astype(bf16)
        self.each(self.reduce_b2(i), "start")

    def grads_b(self, i):
        self.add_cores(i)
        self.each(self.reduce_b(i), "start")

    def grads_c(self, i):
        layer, t, buf, cols = ITEMS[i]
        half = self.Z // 2
        if i == LAST:
            self.each(self.reduce_b(i), "wait")
            total = self.gb[t, self.gy, self.gx, :, self.c, :, cols].astype(f32)
            for k in range(GROUPS - 1):
                total = total + self.rb[k].astype(f32)
            self.sc[buf, :, :, cols] = total.astype(bf16)
        else:
            self.each(self.reduce_b2(i), "wait")
            for j in range(2):
                span = slice(j * half, (j + 1) * half)
                total = self.gb[t, self.gy, self.gx, span, self.c, :, cols].astype(f32)
                total = total + self.rb2[buf, j, :, :, cols].astype(f32)
                self.sc[buf, span, :, cols] = total.astype(bf16)
        self.each(self.reduce_c(i), "start")

    def grads_d(self, i):
        layer, t, buf, cols = ITEMS[i]
        self.each(self.reduce_c(i), "wait")
        total = self.sc[buf, self.z, :, cols].astype(f32)
        for k in range(self.Z - 1):
            total = total + self.rc[layer, t, k, :, cols].astype(f32)
        if self.R > 1:
            self.rx_out[layer, t, :, cols] = total.astype(bf16)
            self.each(self.reduce_r(i), "start")
            self.each(self.reduce_r(i), "wait")
            for j in range(self.R - 1):
                total = total + self.rx[layer, t, j, :, cols].astype(f32)
        self.fin[layer, t, self.g, self.c, :, cols] = total.astype(bf16)
        self.each(self.reduce_d(i)[0], "start")

    def grads_e(self, i):
        out, into = self.reduce_d(i)
        self.each(into, "wait_recv")
        self.each(out, "wait_send")
        self.each(self.reduce_e(i)[0], "start")

    def grads_f(self, i):
        out, into = self.reduce_e(i)
        self.each(into, "wait_recv")
        self.each(out, "wait_send")
        if ITEMS[i][2] < 3:
            self.store(*ITEMS[i][:2]).start()

    def store(self, layer, t):
        return pltpu.make_async_copy(
            self.fin.at[layer, t], self.grads_out.at[layer, t], self.out_sem.at[2 + 3 * layer + t]
        )


    def chunks(self, body, unroll=1):
        loop(self.T // CHUNK, lambda i: body(pl.ds(pl.multiple_of(i * CHUNK, CHUNK), CHUNK)), unroll)

    def spread(self, index):
        column = self.gcol[index].astype(f32)
        return jnp.concatenate([column] * (CHUNK // 128), axis=1)

    def normed(self, x, slot, at):
        mean = jnp.sum(x, axis=0, keepdims=True) * (1.0 / D)
        centered = x - mean
        inverse = lax.rsqrt(
            jnp.sum(centered * centered, axis=0, keepdims=True) * (1.0 / D) + EPS_NORM
        )
        self.stats[2 * slot : 2 * slot + 1, at] = mean
        self.stats[2 * slot + 1 : 2 * slot + 2, at] = inverse
        return centered * inverse

    def norm_back(self, grad, slot, at):
        mean = self.stats[2 * slot : 2 * slot + 1, at]
        inverse = self.stats[2 * slot + 1 : 2 * slot + 2, at]
        normed = (self.xs[slot, :, at] - mean) * inverse
        product = grad * normed
        partial = product[:, 0:128]
        for j in range(1, CHUNK // 128):
            partial = partial + product[:, j * 128 : (j + 1) * 128]
        self.gacc[slot] += partial
        gain = self.spread(slot)
        scaled = grad * gain
        average = jnp.sum(scaled, axis=0, keepdims=True) * (1.0 / D)
        along = jnp.sum(product * gain, axis=0, keepdims=True) * (1.0 / D)
        return inverse * (scaled - average - normed * along)

    def w_qkv(self, layer):
        return self.wqp[layer, :, :, :, 0 : 3 * D].reshape(D, 3 * D)

    def w_proj(self, layer):
        return self.wqp[layer, :, :, :, 3 * D : 4 * D].reshape(D, D)

    def w_up(self, layer):
        return self.wup[layer].reshape(D, FF)

    def w_down(self, layer):
        return self.wdn[layer].reshape(FF, D)

    def make_bias(self):
        prefix, valid = self.prefix[0], self.valid[0]
        key = lax.broadcasted_iota(jnp.int32, (BLOCK, BLOCK), 0)
        query = lax.broadcasted_iota(jnp.int32, (BLOCK, BLOCK), 1)
        causal = key <= query
        fill = lambda ok: jnp.where(ok, f32(0.0), f32(NEG_FILL))
        self.bias[0] = fill(causal | (key < prefix))
        self.bias[1] = fill(causal)
        self.bias[2] = fill(causal & (key + 2 * BLOCK < valid))
        self.bias[3] = fill(causal & (key + 3 * BLOCK < valid))
        self.bias[4] = fill(key + 2 * BLOCK < valid)

    def score_blocks(self, keys_t, queries, q):
        blocks = []
        for j in range(q + 1):
            s = dot(keys_t[j * BLOCK : (j + 1) * BLOCK], queries, 1, 0)
            if j == q:
                s = s + self.bias[q]
            elif j == 2:
                s = s + self.bias[4]
            blocks.append(s)
        return blocks

    def head_rows(self, h, part):
        return pl.ds(pl.multiple_of(part * D + h * HEAD_DIM, HEAD_DIM), HEAD_DIM)

    def attend(self, layer, heads):
        count = self.T // BLOCK
        span = lambda q: slice(q * BLOCK, (q + 1) * BLOCK)
        queries = [self.qkv[layer, self.head_rows(h, 0), :] for h in heads]
        keys_t = [self.qkv[layer, self.head_rows(h, 1), :].T for h in heads]
        ones = jnp.ones((16, self.T), bf16)
        values = [
            jnp.concatenate([self.qkv[layer, self.head_rows(h, 2), :], ones], axis=0) for h in heads
        ]

        def scores(a, q):
            return self.score_blocks(keys_t[a], queries[a][:, span(q)], q)

        def soften(blocks):
            largest = functools.reduce(
                jnp.maximum, [jnp.max(s, axis=0, keepdims=True) for s in blocks]
            )
            probs = jnp.concatenate([jnp.exp(s - largest).astype(bf16) for s in blocks], axis=0)
            return largest, probs

        def mix(a, q, largest, probs):
            mixed = dot(values[a][:, : (q + 1) * BLOCK], probs, 1, 0)
            denominator = mixed[HEAD_DIM : HEAD_DIM + 1]
            mixed = mixed[:HEAD_DIM] * (1.0 / denominator)
            self.om[layer, self.head_rows(heads[a], 0), span(q)] = mixed.astype(bf16)
            self.lse[layer, pl.ds(heads[a], 1), span(q)] = largest + jnp.log(denominator)

        self.pipeline(len(heads), range(count), scores, lambda a, q, s: soften(s), mix)

    def pipeline(self, n, order, first, second, third):
        work = [(a, q) for q in order for a in range(n)]
        now = first(*work[0])
        last = None
        for i, place in enumerate(work):
            ahead = first(*work[i + 1]) if i + 1 < len(work) else None
            made = second(*place, now)
            if last is not None:
                third(*last[0], *last[1])
            last, now = (place, made), ahead
        third(*last[0], *last[1])

    def attend_back(self, layer, heads):
        count = self.T // BLOCK
        span = lambda q: slice(q * BLOCK, (q + 1) * BLOCK)
        part = lambda i: [self.qkv[layer, self.head_rows(h, i), :] for h in heads]
        queries, keys, values = part(0), part(1), part(2)
        keys_t, values_t = [k.T for k in keys], [v.T for v in values]
        grads = [self.dmix[self.head_rows(h, 0), :] for h in heads]
        delta = [
            jnp.sum(
                g.astype(f32) * self.om[layer, self.head_rows(h, 0), :].astype(f32),
                axis=0, keepdims=True,
            )
            for g, h in zip(grads, heads)
        ]
        key_grads = [[None] * count for h in heads]
        value_grads = [[None] * count for h in heads]

        def first(a, q):
            scores = self.score_blocks(keys_t[a], queries[a][:, span(q)], q)
            slopes = [dot(values_t[a][span(j)], grads[a][:, span(q)], 1, 0) for j in range(q + 1)]
            return scores, slopes

        def second(a, q, made):
            total = self.lse[layer, pl.ds(heads[a], 1), span(q)]
            low, small = [], []
            for s, slope in zip(*made):
                probs = jnp.exp(s - total)
                low.append(probs.astype(bf16))
                small.append((probs * (slope - delta[a][:, span(q)])).astype(bf16))
            return jnp.concatenate(low, axis=0), jnp.concatenate(small, axis=0)

        def third(a, q, probs, d_scores):
            k_part = dot(queries[a][:, span(q)], d_scores, 1, 1)
            v_part = dot(grads[a][:, span(q)], probs, 1, 1)
            for j in range(q + 1):
                for grad, more in ((key_grads[a], k_part), (value_grads[a], v_part)):
                    grad[j] = more[:, span(j)] if grad[j] is None else grad[j] + more[:, span(j)]
            q_part = dot(keys[a][:, : (q + 1) * BLOCK], d_scores, 1, 0) * (HEAD_DIM**-0.5)
            self.dqkv[self.head_rows(heads[a], 0), span(q)] = q_part.astype(bf16)

        self.pipeline(len(heads), reversed(range(count)), first, second, third)
        for a, h in enumerate(heads):
            self.dqkv[self.head_rows(h, 1), :] = jnp.concatenate(key_grads[a], axis=1).astype(bf16)
            self.dqkv[self.head_rows(h, 2), :] = jnp.concatenate(value_grads[a], axis=1).astype(bf16)

    def first_norm(self, layer):
        slot = 2 * layer

        def body(at):
            n = self.normed(self.xs[slot, :, at], slot, at)
            self.an[layer, :, at] = (n * self.spread(slot)).astype(bf16)

        self.chunks(body)

    def project_in(self, layer):
        def body(at):
            rows = dot(self.w_qkv(layer), self.an[layer, :, at], 0, 0)
            self.qkv[layer, 0:D, at] = (rows[0:D] * (HEAD_DIM**-0.5)).astype(bf16)
            self.qkv[layer, D : 3 * D, at] = rows[D:].astype(bf16)

        self.chunks(body)

    def middle(self, layer):
        slot = 2 * layer + 1

        def body(at):
            x = self.xs[slot - 1, :, at] + dot(self.w_proj(layer), self.om[layer, :, at], 0, 0)
            self.xs[slot, :, at] = x
            n = self.normed(x, slot, at)
            self.bn[layer, :, at] = (n * self.spread(slot)).astype(bf16)

        self.chunks(body)

    def feed(self, layer):
        def body(at):
            u = dot(self.w_up(layer), self.bn[layer, :, at], 0, 0)
            area = 0.5 + 0.5 * lax.erf(u * (0.5**0.5))
            density = jnp.exp(u * u * (-0.5)) * (1.0 / math.sqrt(2.0 * math.pi))
            hidden = (u * area).astype(bf16)
            self.hid[layer, :, at] = hidden
            self.slope[layer, :, at] = (area + u * density).astype(bf16)
            x = self.xs[2 * layer + 1, :, at] + dot(self.w_down(layer), hidden, 0, 0)
            if layer + 1 < LAYERS:
                self.xs[2 * layer + 2, :, at] = x
            else:
                self.toks[at, :] = x.astype(bf16).T

        self.chunks(body)

    def feed_back(self, layer):
        slot = 2 * layer + 1

        def body(at):
            low = self.dy[:, at].astype(bf16)
            self.dm[:, at] = low
            d_hidden = dot(self.w_down(layer), low, 1, 0)
            d_pre = (d_hidden * self.slope[layer, :, at].astype(f32)).astype(bf16)
            self.slope[layer, :, at] = d_pre
            grad = dot(self.w_up(layer), d_pre, 1, 0)
            total = self.dy[:, at] + self.norm_back(grad, slot, at)
            self.dy[:, at] = total
            low = total.astype(bf16)
            self.datt[:, at] = low
            self.dmix[:, at] = dot(self.w_proj(layer), low, 1, 0).astype(bf16)

        self.chunks(body)

    def down_grad(self, layer):
        width = FF // self.Z

        def body(z):
            rows = self.hid[layer, pl.ds(pl.multiple_of(z * width, 64), width), :]
            value = dot(rows, self.dm[...], 1, 1).astype(bf16)
            self.gb[DOWN, :, :, z] = value.reshape(2, 2, CORES, self.UR, D)

        loop(self.Z, body)

    def store_grad(self, t, g, value):
        self.gb[t, g // 2, g % 2] = value.astype(bf16).reshape(self.Z, CORES, self.UR, D)

    def up_grad(self, layer):
        def body(g):
            rows = self.slope[layer, pl.ds(pl.multiple_of(g * D, 64), D), :]
            self.store_grad(UP, g, dot(self.bn[layer], rows, 1, 1))

        loop(GROUPS, body)

    def proj_grad(self, layer):
        self.store_grad(QP, 3, dot(self.om[layer], self.datt[...], 1, 1))

    def qkv_grad(self, layer):
        def body(g):
            rows = self.dqkv[pl.ds(pl.multiple_of(g * D, 64), D), :]
            self.store_grad(QP, g, dot(self.an[layer], rows, 1, 1))

        loop(3, body)

    def pair_grad(self, p):
        rows = [self.dqkv[g * D + p * PAIR : g * D + (p + 1) * PAIR, :] for g in range(3)]
        value = dot(self.an[0], jnp.concatenate(rows, axis=0), 1, 1).astype(bf16)
        value = value.reshape(self.Z, CORES, self.UR, 3 * PAIR)
        for g in range(3):
            part = value[:, :, :, g * PAIR : (g + 1) * PAIR]
            self.gb[QP, g // 2, g % 2, :, :, :, p * PAIR : (p + 1) * PAIR] = part

    def qkv_back(self, layer):
        slot = 2 * layer

        def body(at):
            grad = dot(self.w_qkv(layer), self.dqkv[:, at], 1, 0)
            total = self.dy[:, at] + self.norm_back(grad, slot, at)
            self.dy[:, at] = total
            if layer == 0:
                self.cots[at, :] = total.astype(bf16).T

        self.chunks(body)


    def gain_slots(self):
        out, into = [], []
        for k, peer in enumerate(self.z_peers):
            mine, theirs = self.gslot.at[self.z], self.gslot.at[self.z_others[k]]
            out.append(self.remote(mine, mine, self.ns.at[k], self.nr.at[k], peer))
            into.append(self.remote(theirs, theirs, self.ns.at[k], self.nr.at[k], peer))
        return out, into

    def gain_stages(self):
        stages = [[self.core_peer], self.group_peers, self.z_peers]
        return stages + [self.r_peers] if self.R > 1 else stages

    def swap_gains(self, stage):
        stages = self.gain_stages()
        at = sum(len(peers) for peers in stages[:stage])
        return [
            self.remote(
                self.nsum.at[stage], self.nin.at[at + k],
                self.ns.at[self.Z - 1 + at + k], self.nr.at[self.Z - 1 + at + k], peer,
            )
            for k, peer in enumerate(stages[stage])
        ]

    def fold_gains(self, stage):
        stages = self.gain_stages()
        at = sum(len(peers) for peers in stages[:stage])
        self.each(self.swap_gains(stage), "wait")
        total = self.nsum[stage]
        for k in range(len(stages[stage])):
            total = total + self.nin[at + k]
        self.nsum[stage + 1] = total
        if stage + 1 < len(stages):
            self.each(self.swap_gains(stage + 1), "start")


    def run(self):
        Z = self.Z
        loads = [
            pltpu.make_async_copy(src, dst, self.in_sem.at[i])
            for i, (src, dst) in enumerate(
                [(self.tokens, self.toks), (self.cotangent, self.cots)]
                + [
                    pair
                    for layer in range(LAYERS)
                    for pair in (
                        (self.qkv_w.at[layer, self.c], self.sq),
                        (self.proj_w.at[layer, self.c], self.sp),
                        (self.up_w.at[layer, self.c], self.su),
                        (self.down_w.at[layer, :, self.c], self.sd),
                    )
                ]
            )
        ]
        for i in (2, 3, 0, 4, 5, 1):
            loads[i].start()
        self.gslot[...] = jnp.zeros_like(self.gslot)
        for layer in range(LAYERS):
            rounded = self.gains[layer].astype(bf16).astype(f32)
            self.gslot[self.z, 2 * layer : 2 * layer + 2, 0 : D // Z] = rounded
        self.gacc[...] = jnp.zeros_like(self.gacc)

        def take_weights(m):
            layer, kind = divmod(m, 3)
            at = 2 + 4 * layer
            parts = [at, at + 1] if kind == QP else [at + 1 + kind]
            for i in parts:
                loads[i].wait()
            if kind == QP:
                self.wqp[layer, self.z, self.c, :, 0 : 3 * D] = self.sq[...].astype(bf16)
                self.wqp[layer, self.z, self.c, :, 3 * D : 4 * D] = self.sp[...].astype(bf16)
            elif kind == UP:
                self.wup[layer, self.z, self.c] = self.su[...].astype(bf16)
            else:
                self.wdn[layer, self.z, :, self.c] = self.sd[...].astype(bf16)
            if layer + 1 < LAYERS:
                for i in parts:
                    loads[i + 4].start()

        take_weights(0)
        barrier = pltpu.get_barrier_semaphore()
        peers = [self.core_peer] + self.group_peers + self.z_peers + self.r_peers
        for peer in peers:
            pl.semaphore_signal(barrier, inc=1, device_id=peer, device_id_type=MESH)
        pl.semaphore_wait(barrier, len(peers))

        self.start_z(0)
        for copy in self.gain_slots()[0]:
            copy.start()
        loads[0].wait()

        def take(at):
            self.xs[0, :, at] = self.toks[at, :].T.astype(f32)

        self.chunks(take)
        self.start_g(0)
        take_weights(1)
        self.start_z(1)
        take_weights(2)
        self.start_z(2)
        for copy in self.gain_slots()[1]:
            copy.wait_recv()
        for copy in self.gain_slots()[0]:
            copy.wait_send()
        for z in range(Z):
            tall = jnp.concatenate([self.gslot[z]] * 16, axis=0).T
            for i in range(2 * LAYERS):
                self.gcol[i, z * (D // Z) : (z + 1) * (D // Z), :] = jnp.broadcast_to(
                    tall[0 : D // Z, i : i + 1], (D // Z, 128)
                ).astype(bf16)
        self.first_norm(0)
        self.start_c(0)
        self.make_bias()
        for m in range(3, 3 * LAYERS):
            take_weights(m)
        self.start_g(1)
        self.start_z(3)
        self.ready(0)
        self.project_in(0)
        self.start_g(2)
        self.start_z(4)
        self.start_z(5)

        def heads(body, layer, n, hooks):
            def step(i):
                body(layer, [n * i + a for a in range(n)])
                for at, hook in hooks:
                    pl.when(i == at)(hook)

            loop(HEADS // n, step)

        def do(f, *args):
            return lambda: f(*args)

        heads(self.attend, 0, 3, [(0, do(self.start_g, 3)), (1, do(self.start_c, 1))])
        self.start_g(4)
        self.ready(1)
        self.middle(0)
        self.start_c(2)
        self.start_g(5)
        self.ready(2)
        self.feed(0)
        self.start_c(3)
        self.first_norm(1)
        self.ready(3)
        self.project_in(1)
        heads(self.attend, 1, 3, [(0, do(self.start_c, 4)), (1, do(self.start_c, 5))])
        self.ready(4)
        self.middle(1)
        self.ready(5)
        self.feed(1)
        out_copy = pltpu.make_async_copy(self.toks, self.block_out, self.out_sem.at[0])
        out_copy.start()
        self.gather_sent()

        loads[1].wait()
        valid = self.valid[0]

        def start_back(at):
            where = at.start + lax.broadcasted_iota(jnp.int32, (D, CHUNK), 1)
            grad = self.cots[at, :].T.astype(f32)
            self.dy[:, at] = jnp.where(where < valid, grad, f32(0.0))

        self.chunks(start_back)

        self.feed_back(1)
        self.down_grad(1)
        self.grads_a(D1)
        self.up_grad(1)
        self.grads_a(U1)
        self.grads_b1(D1)
        self.proj_grad(1)
        heads(
            self.attend_back, 1, 2,
            [
                (0, do(self.grads_b1, U1)),
                (1, do(self.grads_b2, D1)),
                (2, do(self.grads_b2, U1)),
                (2, do(self.grads_c, D1)),
            ],
        )
        self.grads_c(U1)
        self.qkv_grad(1)
        self.grads_a(Q1)
        self.grads_d(D1)
        self.qkv_back(1)
        self.grads_b1(Q1)

        self.feed_back(0)
        self.grads_d(U1)
        self.grads_e(D1)
        self.grads_b2(Q1)
        self.down_grad(0)
        self.grads_f(D1)
        self.grads_a(D0)
        self.up_grad(0)
        self.grads_e(U1)
        self.grads_c(Q1)
        self.grads_b1(D0)
        self.proj_grad(0)
        heads(
            self.attend_back, 0, 2,
            [
                (0, do(self.pair_grad, 0)),
                (0, do(self.grads_a, P0)),
                (0, do(self.grads_f, U1)),
                (0, do(self.grads_a, U0)),
                (0, do(self.grads_d, Q1)),
                (1, do(self.pair_grad, 1)),
                (1, do(self.grads_a, P1)),
                (1, do(self.grads_b2, D0)),
                (1, do(self.grads_b1, U0)),
                (1, do(self.grads_b1, P0)),
                (2, do(self.pair_grad, 2)),
                (2, do(self.grads_a, P2)),
                (2, do(self.grads_e, Q1)),
                (2, do(self.grads_b2, U0)),
                (2, do(self.grads_c, D0)),
                (2, do(self.grads_b1, P1)),
                (2, do(self.grads_b2, P0)),
                (2, do(self.grads_b, P2)),
            ],
        )
        self.qkv_back(0)
        grad_copy = pltpu.make_async_copy(self.cots, self.tokens_grad, self.out_sem.at[1])
        grad_copy.start()

        lane = lax.broadcasted_iota(jnp.int32, (D, 128), 1)
        tall = jnp.zeros((D, 128), f32)
        for i in range(2 * LAYERS):
            column = jnp.sum(self.gacc[i], axis=1, keepdims=True)
            tall = tall + jnp.where(lane == i, column, f32(0.0))
        self.nsum[0] = tall.T[0:8]
        self.each(self.swap_gains(0), "start")
        self.grads_b2(P1)
        self.grads_c(U0)
        self.grads_c(P0)
        self.fold_gains(0)
        self.grads_f(Q1)
        self.grads_c(P2)
        self.grads_d(D0)
        self.grads_c(P1)
        self.grads_d(U0)
        self.fold_gains(1)
        self.grads_e(D0)
        self.grads_d(P0)
        self.grads_d(P2)
        self.grads_d(P1)
        self.grads_e(U0)
        self.fold_gains(2)
        if self.R > 1:
            self.fold_gains(3)
        tall = jnp.concatenate([self.nsum[len(self.gain_stages())]] * 16, axis=0).T
        self.gacc[0] = tall
        width = D // Z
        mine = self.gacc[0, pl.ds(pl.multiple_of(self.z * width, 8), width), :]
        mine = jnp.concatenate([mine, jnp.zeros((128 - width, 128), f32)], axis=0).T
        self.gains_grad[...] = mine[0:8]
        self.grads_f(D0)
        self.grads_f(U0)
        for i in (P0, P2, P1):
            self.grads_e(i)
        for i in (P0, P2, P1):
            self.grads_f(i)
        self.store(0, QP).start()
        out_copy.wait()
        grad_copy.wait()
        for layer in range(LAYERS):
            for t in range(3):
                self.store(layer, t).wait()


def adam(weight, first, second, grad, rate, decay):
    first_new = BETA_ONE * first + (1.0 - BETA_ONE) * grad
    second_new = BETA_TWO * second + (1.0 - BETA_TWO) * grad * grad
    first_fix = 1.0 - BETA_ONE**STEP_COUNT
    second_fix = 1.0 - BETA_TWO**STEP_COUNT
    update = first_new / first_fix / (jnp.sqrt(second_new / second_fix) + EPS_ADAM)
    return first_new, second_new, weight - rate * (update + decay * weight)


def adam_kernel(*refs):
    (block_in, tgrad_in, grads, gains_grad) = refs[:4]
    masters = refs[4:19]
    block_out, tgrad_out = refs[19:21]
    outs = refs[21:]
    rates = (
        2.5 / math.sqrt(D),
        2.5 / math.sqrt(max(4 * D // SEQ, 1)),
        2.5 / math.sqrt(D),
        2.5 / math.sqrt(FF),
        0.5,
    )
    block_out[...] = block_in[...]
    tgrad_out[...] = tgrad_in[...]

    def update(kind, index, grad):
        weight, first, second = (masters[3 * kind + j] for j in range(3))
        new = adam(
            weight[index], first[index], second[index], grad, rates[kind],
            0.1 if kind < 4 else 0.0,
        )
        for j in range(3):
            outs[3 * kind + j][index] = new[j]

    for g in range(GROUPS):
        grad = grads[0, QP, g, 0].astype(f32)
        if g < 3:
            update(0, (0, 0, slice(None), slice(g * D, (g + 1) * D)), grad)
        else:
            update(1, (0, 0), grad)
        update(2, (0, 0, slice(None), slice(g * D, (g + 1) * D)), grads[0, UP, g, 0].astype(f32))
        update(3, (0, g, 0), grads[0, DOWN, g, 0].astype(f32))
    width = masters[12].shape[-1]
    for layer in range(LAYERS):
        update(4, (layer,), gains_grad[2 * layer : 2 * layer + 2, 0:width])


def make_per_device(n_dp, n_fsdp):
    Z, R = n_fsdp, n_dp // UNITS
    UR = D // Z // CORES

    def per_device(
        tokens, cotangent, prefix_len, valid_len,
        qkv_weight, qkv_first, qkv_second,
        proj_weight, proj_first, proj_second,
        up_weight, up_first, up_second,
        down_weight, down_first, down_second,
        norm_gains, gains_first, gains_second,
    ):
        T = tokens.shape[0]
        assert prefix_len.shape == (1,) and T == 4 * BLOCK
        assert FF // Z // UNITS == UR
        rows4 = lambda w: w.reshape(LAYERS, CORES, UR, w.shape[-1])
        rows5 = lambda w: w.reshape(LAYERS, GROUPS, CORES, UR, D)
        vmem = pltpu.VMEM
        scratch = dict(
            wqp=vmem((LAYERS, Z, CORES, UR, 4 * D), bf16),
            wup=vmem((LAYERS, Z, CORES, UR, FF), bf16),
            wdn=vmem((LAYERS, Z, GROUPS, CORES, UR, D), bf16),
            sq=vmem((UR, 3 * D), f32),
            sp=vmem((UR, D), f32),
            su=vmem((UR, FF), f32),
            sd=vmem((GROUPS, UR, D), f32),
            gslot=vmem((Z, 8, 128), f32),
            gcol=vmem((2 * LAYERS, D, 128), bf16),
            gacc=vmem((2 * LAYERS, D, 128), f32),
            xs=vmem((2 * LAYERS, D, T), f32),
            dy=vmem((D, T), f32),
            an=vmem((LAYERS, D, T), bf16),
            bn=vmem((LAYERS, D, T), bf16),
            qkv=vmem((LAYERS, 3 * D, T), bf16),
            om=vmem((LAYERS, D, T), bf16),
            hid=vmem((LAYERS, FF, T), bf16),
            slope=vmem((LAYERS, FF, T), bf16),
            dqkv=vmem((3 * D, T), bf16),
            dmix=vmem((D, T), bf16),
            dm=vmem((D, T), bf16),
            datt=vmem((D, T), bf16),
            lse=vmem((LAYERS, 8, T), f32),
            stats=vmem((4 * LAYERS, T), f32),
            bias=vmem((5, BLOCK, BLOCK), f32),
            toks=vmem((T, D), bf16),
            cots=vmem((T, D), bf16),
            gb=vmem((3, 2, 2, Z, CORES, UR, D), bf16),
            ra=vmem((4, 2, 2, Z, UR, D), bf16),
            rb1=vmem((4, 2, 2, Z // 2, UR, D), bf16),
            rb2=vmem((4, 2, Z // 2, UR, D), bf16),
            rb=vmem((GROUPS - 1, Z, UR, PAIR), bf16),
            sc=vmem((4, Z, UR, D), bf16),
            rc=vmem((LAYERS, 3, Z - 1, UR, D), bf16),
            fin=vmem((LAYERS, 3, GROUPS, CORES, UR, D), bf16),
            nsum=vmem((5, 8, D), f32),
            nin=vmem((GROUPS + Z + R - 2, 8, D), f32),
        )
        sem = pltpu.SemaphoreType.DMA
        scratch.update(
            zs=sem((3 * LAYERS, Z - 1)),
            zr=sem((3 * LAYERS, Z - 1)),
            gs=sem((3 * LAYERS, 3 * (Z - 1))),
            gr=sem((3 * LAYERS, 3 * (Z - 1))),
            cs=sem((3 * LAYERS, Z)),
            cr=sem((3 * LAYERS, Z)),
            rs=sem((len(ITEMS), 8 + Z)),
            rr=sem((len(ITEMS), 8 + Z)),
            ns=sem((2 * Z + R + 4,)),
            nr=sem((2 * Z + R + 4,)),
            in_sem=sem((2 + 4 * LAYERS,)),
            out_sem=sem((2 + 3 * LAYERS,)),
        )
        if R > 1:
            scratch.update(
                rx=vmem((LAYERS, 3, R - 1, UR, D), bf16),
                rx_out=vmem((LAYERS, 3, UR, D), bf16),
                rxs=sem((len(ITEMS), R - 1)),
                rxr=sem((len(ITEMS), R - 1)),
            )
        ins = dict(
            tokens=tokens, cotangent=cotangent, prefix=prefix_len, valid=valid_len,
            qkv_w=rows4(qkv_weight), proj_w=rows4(proj_weight), up_w=rows4(up_weight),
            down_w=rows5(down_weight), gains=norm_gains,
        )
        outs = dict(
            block_out=jax.ShapeDtypeStruct((T, D), bf16),
            tokens_grad=jax.ShapeDtypeStruct((T, D), bf16),
            grads_out=jax.ShapeDtypeStruct((LAYERS, 3, GROUPS, CORES, UR, D), bf16),
            gains_grad=jax.ShapeDtypeStruct((8, 128), f32),
        )
        names = list(ins) + list(outs) + list(scratch)
        hbm = pl.BlockSpec(memory_space=pl.ANY)
        smem = pl.BlockSpec(memory_space=pltpu.SMEM)
        local = pl.BlockSpec(memory_space=pltpu.VMEM)

        def kernel(*refs):
            Step(dict(T=T, Z=Z, R=R, UR=UR), dict(zip(names, refs))).run()

        block_mid, tgrad_mid, grads, gains_grad = pl.pallas_call(
            kernel,
            out_shape=list(outs.values()),
            in_specs=[hbm, hbm, smem, smem, hbm, hbm, hbm, hbm, local],
            out_specs=[hbm, hbm, hbm, local],
            scratch_shapes=list(scratch.values()),
            compiler_params=pltpu.CompilerParams(
                collective_id=0, has_side_effects=True, vmem_limit_bytes=63 * 1024 * 1024
            ),
            name="train_step",
        )(*ins.values())

        masters = [
            f(w)
            for f, group in (
                (rows4, (qkv_weight, qkv_first, qkv_second)),
                (rows4, (proj_weight, proj_first, proj_second)),
                (rows4, (up_weight, up_first, up_second)),
                (rows5, (down_weight, down_first, down_second)),
                (lambda w: w, (norm_gains, gains_first, gains_second)),
            )
            for w in group
        ]
        tok_block = pl.BlockSpec((T // 4, D), lambda l, c: (2 * l + c, 0))

        def spec(w):
            if w.ndim == 4:
                return pl.BlockSpec((1, 1, *w.shape[2:]), lambda l, c: (l, c, 0, 0))
            if w.ndim == 5:
                return pl.BlockSpec((1, GROUPS, 1, UR, D), lambda l, c: (l, 0, c, 0, 0))
            return pl.BlockSpec(w.shape, lambda l, c: (0, 0, 0))

        specs = [spec(w) for w in masters]
        done = pl.pallas_call(
            adam_kernel,
            grid=(LAYERS, CORES),
            out_shape=[jax.ShapeDtypeStruct((T, D), bf16)] * 2
            + [jax.ShapeDtypeStruct(w.shape, f32) for w in masters],
            in_specs=[
                tok_block,
                tok_block,
                pl.BlockSpec((1, 3, GROUPS, 1, UR, D), lambda l, c: (l, 0, 0, c, 0, 0)),
                pl.BlockSpec((8, 128), lambda l, c: (0, 0)),
                *specs,
            ],
            out_specs=[tok_block, tok_block, *specs],
            compiler_params=pltpu.CompilerParams(vmem_limit_bytes=62 * 1024 * 1024),
            name="adam",
        )(block_mid, tgrad_mid, grads, gains_grad, *masters)
        shapes = [
            w.shape
            for w in (
                qkv_weight, qkv_first, qkv_second, proj_weight, proj_first, proj_second,
                up_weight, up_first, up_second, down_weight, down_first, down_second,
                norm_gains, gains_first, gains_second,
            )
        ]
        news = [x.reshape(s) for x, s in zip(done[2:], shapes)]
        results = []
        for kind in range(5):
            weight_new, second_new, first_new = news[3 * kind + 2], news[3 * kind + 1], news[3 * kind]
            results += [first_new, second_new, weight_new]
        return (done[0], done[1], *results)

    return per_device


def solution(mesh):
    rows = P(("dp", "fsdp"), None)
    lens = P(("dp", "fsdp"))
    weight = P(None, "fsdp", None)
    gain = P(None, None, "fsdp")
    return jax.shard_map(
        make_per_device(mesh.shape["dp"], mesh.shape["fsdp"]),
        mesh=mesh,
        in_specs=(rows, rows, lens, lens, *([weight] * 12), *([gain] * 3)),
        out_specs=(rows, rows, *([weight] * 12), *([gain] * 3)),
        check_vma=False,
    )
```

```python
import functools
import math

import jax
import jax.numpy as jnp
from jax import lax
from jax.experimental import pallas as pl
from jax.experimental.pallas import tpu as pltpu
from jax.sharding import PartitionSpec as P

D = 384
HEADS = 6
HEAD_DIM = 64
FF = 1536
SEQ = 1024
STEP_COUNT = 7

NEG_FILL = -1e30
EPS_NORM = 1e-05
EPS_ADAM = 1e-08
BETA_ONE = 0.9
BETA_TWO = 0.99

LAYERS = 2
GROUPS = 4
CORES = 2
UNITS = GROUPS * CORES
BLOCK = 256
CHUNK = 512
QP, UP, DOWN = 0, 1, 2
PAIR = 2 * HEAD_DIM
ITEMS = [(layer, kind, kind, pl.ds(0, D)) for layer, kind in ((1, DOWN), (1, UP), (1, QP), (0, DOWN), (0, UP))]
ITEMS += [(0, QP, 3, pl.ds(p * PAIR, PAIR)) for p in range(3)]
D1, U1, Q1, D0, U0, P0, P1, P2 = range(8)
LAST = P2

MESH = pl.DeviceIdType.MESH
bf16 = jnp.bfloat16
f32 = jnp.float32


def dot(left, right, left_dim, right_dim):
    return lax.dot_general(
        left, right, (((left_dim,), (right_dim,)), ((), ())), preferred_element_type=f32
    )


def loop(count, body, unroll=1):
    def step(index, carry):
        body(index)
        return carry

    lax.fori_loop(0, count, step, 0, unroll=unroll)


class Remote:
    def __init__(self, src, dst, send, recv, device):
        self.made = lambda: pltpu.make_async_remote_copy(
            src_ref=src, dst_ref=dst, send_sem=send, recv_sem=recv,
            device_id=device, device_id_type=MESH,
        )

    def start(self):
        self.made().start()

    def wait_send(self):
        self.made().wait_send()

    def wait_recv(self):
        self.made().wait_recv()

    def wait(self):
        self.made().wait()


class Step:
    def __init__(self, sizes, refs):
        self.__dict__.update(sizes)
        self.__dict__.update(refs)
        self.dp = lax.axis_index("dp")
        self.z = lax.axis_index("fsdp")
        self.unit = self.dp % UNITS
        self.c = self.unit % CORES
        self.g = self.unit // CORES
        self.base = self.dp - self.unit
        self.core_peer = (self.base + self.g * CORES + (1 - self.c), self.z)
        gx, gy = self.g % 2, self.g // 2
        self.gx, self.gy = gx, gy
        self.others = [gy * 2 + (1 - gx), (1 - gy) * 2 + gx, (1 - gy) * 2 + (1 - gx)]
        self.group_peers = [(self.base + g * CORES + self.c, self.z) for g in self.others]
        self.z_others = []
        for k in range(1, self.Z):
            other, bit = 0, 1
            while bit < self.Z:
                own = (self.z // bit) % 2
                other = other + bit * (1 - own if k & bit else own)
                bit *= 2
            self.z_others.append(other)
        self.z_peers = [(self.dp, z) for z in self.z_others]
        total = self.R * UNITS
        self.r_peers = [((self.dp + j * UNITS) % total, self.z) for j in range(1, self.R)]


    def remote(self, src, dst, send, recv, device):
        return Remote(src, dst, send, recv, device)

    def weight_unit(self, kind, layer, z, g, c):
        if kind == DOWN:
            return self.wdn.at[layer, z, g, c]
        whole = self.wqp if kind == QP else self.wup
        return whole.at[layer, z, c, :, pl.ds(pl.multiple_of(g * D, 128), D)]

    def weight_half(self, kind, layer, z, c):
        if kind == DOWN:
            return self.wdn.at[layer, z, :, c]
        return (self.wqp if kind == QP else self.wup).at[layer, z, c]

    def settle(self, ref, sem):
        pltpu.make_async_copy(ref, ref, sem).wait()

    def gather_z(self, m):
        layer, kind = divmod(m, 3)
        mine = self.weight_unit(kind, layer, self.z, self.g, self.c)
        arrived = [self.zr.at[k if m == 0 else self.Z - 2 + m] for k in range(self.Z - 1)]
        return [
            self.remote(mine, mine, self.zs.at[0], arrived[k], peer)
            for k, peer in enumerate(self.z_peers)
        ]

    def gather_g(self, m, k):
        layer, kind = divmod(m, 3)
        mine = self.weight_unit(kind, layer, self.z_others[k], self.g, self.c)
        return [
            self.remote(mine, mine, self.gs.at[m], self.gr.at[m, k], peer)
            for peer in self.group_peers
        ]

    def gather_c(self, m, k):
        layer, kind = divmod(m, 3)
        z = self.z if k == self.Z - 1 else self.z_others[k]
        mine = self.weight_half(kind, layer, z, self.c)
        return self.remote(mine, mine, self.cs.at[layer], self.cr.at[m], self.core_peer)

    def start_z(self, m):
        self.each(self.gather_z(m), "start")
        self.gather_c(m, self.Z - 1).start()

    def start_g(self, m):
        if m > 0:
            self.settle(self.rc.at[0, 0], self.zr.at[self.Z - 2 + m])
        for k in range(self.Z - 1):
            if m == 0:
                self.settle(self.rc.at[0, 0, 0], self.zr.at[k])
            self.each(self.gather_g(m, k), "start")

    def start_c(self, m):
        for k in range(self.Z - 1):
            self.settle(self.rc.at[0, 0], self.gr.at[m, k])
            self.gather_c(m, k).start()

    def ready(self, m):
        self.settle(self.fin.at[0, 0:2], self.cr.at[m])

    def gather_sent(self):
        self.settle(self.fin.at[0, :, 0:3], self.zs.at[0])
        for m in range(3 * LAYERS):
            self.settle(self.rc.at[0], self.gs.at[m])
        for layer in range(LAYERS):
            self.settle(self.fin, self.cs.at[layer])


    def reduce_a(self, i):
        layer, t, buf, cols = ITEMS[i]
        return self.remote(
            self.gb.at[t, :, :, :, 1 - self.c, :, cols], self.ra.at[buf, :, :, :, :, cols],
            self.rs.at[i, 0], self.rr.at[i, 0], self.core_peer,
        )

    def reduce_b1(self, i):
        layer, t, buf, cols = ITEMS[i]
        half = self.Z // 2
        return [
            self.remote(
                self.gb.at[t, :, 1 - self.gx, 0:half, self.c, :, cols],
                self.rb1.at[buf, 0, :, :, :, cols],
                self.rs.at[i, 1], self.rr.at[i, 1], self.group_peers[0],
            ),
            self.remote(
                self.gb.at[t, 1 - self.gy, :, half:, self.c, :, cols],
                self.rb1.at[buf, 1, :, :, :, cols],
                self.rs.at[i, 1], self.rr.at[i, 1], self.group_peers[1],
            ),
        ]

    def reduce_b2(self, i):
        layer, t, buf, cols = ITEMS[i]
        half = self.Z // 2
        return [
            self.remote(
                self.gb.at[t, 1 - self.gy, self.gx, 0:half, self.c, :, cols],
                self.rb2.at[buf, 0, :, :, cols],
                self.rs.at[i, 2], self.rr.at[i, 2], self.group_peers[1],
            ),
            self.remote(
                self.gb.at[t, self.gy, 1 - self.gx, half:, self.c, :, cols],
                self.rb2.at[buf, 1, :, :, cols],
                self.rs.at[i, 2], self.rr.at[i, 2], self.group_peers[0],
            ),
        ]

    def reduce_b(self, i):
        layer, t, buf, cols = ITEMS[i]
        return [
            self.remote(
                self.gb.at[t, self.others[k] // 2, self.others[k] % 2, :, self.c, :, cols],
                self.rb.at[k],
                self.rs.at[i, 1], self.rr.at[i, 1], peer,
            )
            for k, peer in enumerate(self.group_peers)
        ]

    def reduce_c(self, i):
        layer, t, buf, cols = ITEMS[i]
        return [
            self.remote(
                self.sc.at[buf, self.z_others[k], :, cols], self.rc.at[layer, t, k, :, cols],
                self.rs.at[i, 3], self.rr.at[i, 3], peer,
            )
            for k, peer in enumerate(self.z_peers)
        ]

    def reduce_r(self, i):
        layer, t, buf, cols = ITEMS[i]
        return [
            self.remote(
                self.rx_out.at[layer, t, :, cols], self.rx.at[layer, t, j, :, cols],
                self.rxs.at[i], self.rxr.at[i], peer,
            )
            for j, peer in enumerate(self.r_peers)
        ]

    def reduce_d(self, i):
        layer, t, buf, cols = ITEMS[i]
        mine = self.fin.at[layer, t, self.g, self.c, :, cols]
        return [
            self.remote(mine, mine, self.rs.at[i, 4], self.rr.at[i, 4], peer)
            for peer in self.group_peers
        ]

    def reduce_e(self, i):
        layer, t, buf, cols = ITEMS[i]
        mine = self.fin.at[layer, t, :, self.c, :, cols]
        return self.remote(mine, mine, self.rs.at[i, 5], self.rr.at[i, 5], self.core_peer)

    def settle_both(self, ref, i, stage):
        self.settle(ref, self.rs.at[i, stage])
        self.settle(ref, self.rr.at[i, stage])

    def each(self, copies, action):
        for copy in copies:
            getattr(copy, action)()

    def grads_a(self, i):
        self.reduce_a(i).start()

    def add_cores(self, i):
        layer, t, buf, cols = ITEMS[i]
        self.settle_both(self.ra.at[buf, :, :, :, :, cols], i, 0)

        def add(g):
            at = (t, g // 2, g % 2, slice(None), self.c, slice(None), cols)
            both = self.gb[at].astype(f32) + self.ra[buf, g // 2, g % 2, :, :, cols].astype(f32)
            self.gb[at] = both.astype(bf16)

        loop(GROUPS, add)

    def grads_b1(self, i):
        self.add_cores(i)
        self.each(self.reduce_b1(i), "start")

    def grads_b2(self, i):
        layer, t, buf, cols = ITEMS[i]
        half = self.Z // 2
        self.settle_both(self.rb1.at[buf, :, :, :, :, cols], i, 1)
        at = (t, slice(None), self.gx, slice(0, half), self.c, slice(None), cols)
        both = self.gb[at].astype(f32) + self.rb1[buf, 0, :, :, :, cols].astype(f32)
        self.gb[at] = both.astype(bf16)
        at = (t, self.gy, slice(None), slice(half, self.Z), self.c, slice(None), cols)
        both = self.gb[at].astype(f32) + self.rb1[buf, 1, :, :, :, cols].astype(f32)
        self.gb[at] = both.astype(bf16)
        self.each(self.reduce_b2(i), "start")

    def grads_b(self, i):
        self.add_cores(i)
        self.each(self.reduce_b(i), "start")

    def grads_c(self, i):
        layer, t, buf, cols = ITEMS[i]
        half = self.Z // 2
        if i == LAST:
            self.settle_both(self.rb, i, 1)
            total = self.gb[t, self.gy, self.gx, :, self.c, :, cols].astype(f32)
            for k in range(GROUPS - 1):
                total = total + self.rb[k].astype(f32)
            self.sc[buf, :, :, cols] = total.astype(bf16)
        else:
            self.settle_both(self.rb2.at[buf, :, :, :, cols], i, 2)
            for j in range(2):
                span = slice(j * half, (j + 1) * half)
                total = self.gb[t, self.gy, self.gx, span, self.c, :, cols].astype(f32)
                total = total + self.rb2[buf, j, :, :, cols].astype(f32)
                self.sc[buf, span, :, cols] = total.astype(bf16)
        self.each(self.reduce_c(i), "start")

    def grads_d(self, i):
        layer, t, buf, cols = ITEMS[i]
        self.settle_both(self.rc.at[layer, t, :, :, cols], i, 3)
        total = self.sc[buf, self.z, :, cols].astype(f32)
        for k in range(self.Z - 1):
            total = total + self.rc[layer, t, k, :, cols].astype(f32)
        if self.R > 1:
            self.rx_out[layer, t, :, cols] = total.astype(bf16)
            self.each(self.reduce_r(i), "start")
            self.settle(self.rx.at[layer, t, :, :, cols], self.rxs.at[i])
            self.settle(self.rx.at[layer, t, :, :, cols], self.rxr.at[i])
            for j in range(self.R - 1):
                total = total + self.rx[layer, t, j, :, cols].astype(f32)
        self.fin[layer, t, self.g, self.c, :, cols] = total.astype(bf16)
        self.each(self.reduce_d(i), "start")

    def grads_e(self, i):
        layer, t, buf, cols = ITEMS[i]
        self.settle_both(self.rc.at[layer, t, :, :, cols], i, 4)
        self.reduce_e(i).start()

    def grads_f(self, i):
        layer, t, buf, cols = ITEMS[i]
        self.settle_both(self.fin.at[layer, t, :, 1 - self.c, :, cols], i, 5)
        if buf < 3:
            self.store(layer, t).start()

    def store(self, layer, t):
        return pltpu.make_async_copy(
            self.fin.at[layer, t], self.grads_out.at[layer, t], self.out_sem.at[2 + 3 * layer + t]
        )


    def chunks(self, body, unroll=1):
        loop(self.T // CHUNK, lambda i: body(pl.ds(pl.multiple_of(i * CHUNK, CHUNK), CHUNK)), unroll)

    def spread(self, index):
        column = self.gcol[index].astype(f32)
        return jnp.concatenate([column] * (CHUNK // 128), axis=1)

    def normed(self, x, slot, at):
        mean = jnp.sum(x, axis=0, keepdims=True) * (1.0 / D)
        centered = x - mean
        inverse = lax.rsqrt(
            jnp.sum(centered * centered, axis=0, keepdims=True) * (1.0 / D) + EPS_NORM
        )
        self.stats[2 * slot : 2 * slot + 1, at] = mean
        self.stats[2 * slot + 1 : 2 * slot + 2, at] = inverse
        return centered * inverse

    def norm_back(self, grad, slot, at):
        mean = self.stats[2 * slot : 2 * slot + 1, at]
        inverse = self.stats[2 * slot + 1 : 2 * slot + 2, at]
        normed = (self.xs[slot, :, at] - mean) * inverse
        product = grad * normed
        partial = product[:, 0:128]
        for j in range(1, CHUNK // 128):
            partial = partial + product[:, j * 128 : (j + 1) * 128]
        self.gacc[slot] += partial
        gain = self.spread(slot)
        scaled = grad * gain
        average = jnp.sum(scaled, axis=0, keepdims=True) * (1.0 / D)
        along = jnp.sum(product * gain, axis=0, keepdims=True) * (1.0 / D)
        return inverse * (scaled - average - normed * along)

    def w_qkv(self, layer):
        return self.wqp[layer, :, :, :, 0 : 3 * D].reshape(D, 3 * D)

    def w_proj(self, layer):
        return self.wqp[layer, :, :, :, 3 * D : 4 * D].reshape(D, D)

    def w_up(self, layer):
        return self.wup[layer].reshape(D, FF)

    def w_down(self, layer):
        return self.wdn[layer].reshape(FF, D)

    def make_bias(self):
        prefix, valid = self.prefix[0], self.valid[0]
        key = lax.broadcasted_iota(jnp.int32, (BLOCK, BLOCK), 0)
        query = lax.broadcasted_iota(jnp.int32, (BLOCK, BLOCK), 1)
        causal = key <= query
        fill = lambda ok: jnp.where(ok, f32(0.0), f32(NEG_FILL))
        self.bias[0] = fill(causal | (key < prefix))
        self.bias[1] = fill(causal)
        self.bias[2] = fill(causal & (key + 2 * BLOCK < valid))
        self.bias[3] = fill(causal & (key + 3 * BLOCK < valid))
        self.bias[4] = fill(key + 2 * BLOCK < valid)

    def score_blocks(self, keys_t, queries, q):
        blocks = []
        for j in range(q + 1):
            s = dot(keys_t[j * BLOCK : (j + 1) * BLOCK], queries, 1, 0)
            if j == q:
                s = s + self.bias[q]
            elif j == 2:
                s = s + self.bias[4]
            blocks.append(s)
        return blocks

    def head_rows(self, h, part):
        return pl.ds(pl.multiple_of(part * D + h * HEAD_DIM, HEAD_DIM), HEAD_DIM)

    def attend(self, layer, heads):
        count = self.T // BLOCK
        span = lambda q: slice(q * BLOCK, (q + 1) * BLOCK)
        queries = [self.qkv[layer, self.head_rows(h, 0), :] for h in heads]
        keys_t = [self.qkv[layer, self.head_rows(h, 1), :].T for h in heads]
        ones = jnp.ones((16, self.T), bf16)
        values = [
            jnp.concatenate([self.qkv[layer, self.head_rows(h, 2), :], ones], axis=0) for h in heads
        ]

        def scores(a, q):
            return self.score_blocks(keys_t[a], queries[a][:, span(q)], q)

        def soften(blocks):
            largest = functools.reduce(
                jnp.maximum, [jnp.max(s, axis=0, keepdims=True) for s in blocks]
            )
            probs = jnp.concatenate([jnp.exp(s - largest).astype(bf16) for s in blocks], axis=0)
            return largest, probs

        def mix(a, q, largest, probs):
            mixed = dot(values[a][:, : (q + 1) * BLOCK], probs, 1, 0)
            denominator = mixed[HEAD_DIM : HEAD_DIM + 1]
            mixed = mixed[:HEAD_DIM] * (1.0 / denominator)
            self.om[layer, self.head_rows(heads[a], 0), span(q)] = mixed.astype(bf16)
            self.lse[layer, pl.ds(heads[a], 1), span(q)] = largest + jnp.log(denominator)

        self.pipeline(len(heads), range(count), scores, lambda a, q, s: soften(s), mix)

    def pipeline(self, n, order, first, second, third):
        work = [(a, q) for q in order for a in range(n)]
        now = first(*work[0])
        last = None
        for i, place in enumerate(work):
            ahead = first(*work[i + 1]) if i + 1 < len(work) else None
            made = second(*place, now)
            if last is not None:
                third(*last[0], *last[1])
            last, now = (place, made), ahead
        third(*last[0], *last[1])

    def attend_back(self, layer, heads):
        count = self.T // BLOCK
        span = lambda q: slice(q * BLOCK, (q + 1) * BLOCK)
        part = lambda i: [self.qkv[layer, self.head_rows(h, i), :] for h in heads]
        queries, keys, values = part(0), part(1), part(2)
        keys_t, values_t = [k.T for k in keys], [v.T for v in values]
        grads = [self.dmix[self.head_rows(h, 0), :] for h in heads]
        delta = [
            jnp.sum(
                g.astype(f32) * self.om[layer, self.head_rows(h, 0), :].astype(f32),
                axis=0, keepdims=True,
            )
            for g, h in zip(grads, heads)
        ]
        key_grads = [[None] * count for h in heads]
        value_grads = [[None] * count for h in heads]

        def first(a, q):
            scores = self.score_blocks(keys_t[a], queries[a][:, span(q)], q)
            slopes = [dot(values_t[a][span(j)], grads[a][:, span(q)], 1, 0) for j in range(q + 1)]
            return scores, slopes

        def second(a, q, made):
            total = self.lse[layer, pl.ds(heads[a], 1), span(q)]
            low, small = [], []
            for s, slope in zip(*made):
                probs = jnp.exp(s - total)
                low.append(probs.astype(bf16))
                small.append((probs * (slope - delta[a][:, span(q)])).astype(bf16))
            return jnp.concatenate(low, axis=0), jnp.concatenate(small, axis=0)

        def third(a, q, probs, d_scores):
            k_part = dot(queries[a][:, span(q)], d_scores, 1, 1)
            v_part = dot(grads[a][:, span(q)], probs, 1, 1)
            for j in range(q + 1):
                for grad, more in ((key_grads[a], k_part), (value_grads[a], v_part)):
                    grad[j] = more[:, span(j)] if grad[j] is None else grad[j] + more[:, span(j)]
            q_part = dot(keys[a][:, : (q + 1) * BLOCK], d_scores, 1, 0) * (HEAD_DIM**-0.5)
            self.dqkv[self.head_rows(heads[a], 0), span(q)] = q_part.astype(bf16)

        self.pipeline(len(heads), reversed(range(count)), first, second, third)
        for a, h in enumerate(heads):
            self.dqkv[self.head_rows(h, 1), :] = jnp.concatenate(key_grads[a], axis=1).astype(bf16)
            self.dqkv[self.head_rows(h, 2), :] = jnp.concatenate(value_grads[a], axis=1).astype(bf16)

    def first_norm(self, layer):
        slot = 2 * layer

        def body(at):
            n = self.normed(self.xs[slot, :, at], slot, at)
            self.an[layer, :, at] = (n * self.spread(slot)).astype(bf16)

        self.chunks(body)

    def project_in(self, layer):
        def body(at):
            rows = dot(self.w_qkv(layer), self.an[layer, :, at], 0, 0)
            self.qkv[layer, 0:D, at] = (rows[0:D] * (HEAD_DIM**-0.5)).astype(bf16)
            self.qkv[layer, D : 3 * D, at] = rows[D:].astype(bf16)

        self.chunks(body)

    def middle(self, layer):
        slot = 2 * layer + 1

        def body(at):
            x = self.xs[slot - 1, :, at] + dot(self.w_proj(layer), self.om[layer, :, at], 0, 0)
            self.xs[slot, :, at] = x
            n = self.normed(x, slot, at)
            self.bn[layer, :, at] = (n * self.spread(slot)).astype(bf16)

        self.chunks(body)

    def feed(self, layer):
        def body(at):
            u = dot(self.w_up(layer), self.bn[layer, :, at], 0, 0)
            area = 0.5 + 0.5 * lax.erf(u * (0.5**0.5))
            density = jnp.exp(u * u * (-0.5)) * (1.0 / math.sqrt(2.0 * math.pi))
            hidden = (u * area).astype(bf16)
            self.hid[layer, :, at] = hidden
            self.slope[layer, :, at] = (area + u * density).astype(bf16)
            x = self.xs[2 * layer + 1, :, at] + dot(self.w_down(layer), hidden, 0, 0)
            if layer + 1 < LAYERS:
                self.xs[2 * layer + 2, :, at] = x
            else:
                self.toks[at, :] = x.astype(bf16).T

        self.chunks(body)

    def feed_back(self, layer):
        slot = 2 * layer + 1

        def body(at):
            low = self.dy[:, at].astype(bf16)
            self.dm[:, at] = low
            d_hidden = dot(self.w_down(layer), low, 1, 0)
            d_pre = (d_hidden * self.slope[layer, :, at].astype(f32)).astype(bf16)
            self.slope[layer, :, at] = d_pre
            grad = dot(self.w_up(layer), d_pre, 1, 0)
            total = self.dy[:, at] + self.norm_back(grad, slot, at)
            self.dy[:, at] = total
            low = total.astype(bf16)
            self.datt[:, at] = low
            self.dmix[:, at] = dot(self.w_proj(layer), low, 1, 0).astype(bf16)

        self.chunks(body)

    def down_grad(self, layer):
        width = FF // self.Z

        def body(z):
            rows = self.hid[layer, pl.ds(pl.multiple_of(z * width, 64), width), :]
            value = dot(rows, self.dm[...], 1, 1).astype(bf16)
            self.gb[DOWN, :, :, z] = value.reshape(2, 2, CORES, self.UR, D)

        loop(self.Z, body, self.Z)

    def store_grad(self, t, g, value):
        self.gb[t, g // 2, g % 2] = value.astype(bf16).reshape(self.Z, CORES, self.UR, D)

    def up_grad(self, layer):
        def body(g):
            rows = self.slope[layer, pl.ds(pl.multiple_of(g * D, 64), D), :]
            self.store_grad(UP, g, dot(self.bn[layer], rows, 1, 1))

        loop(GROUPS, body, GROUPS)

    def proj_grad(self, layer):
        self.store_grad(QP, 3, dot(self.om[layer], self.datt[...], 1, 1))

    def qkv_grad(self, layer):
        def body(g):
            rows = self.dqkv[pl.ds(pl.multiple_of(g * D, 64), D), :]
            self.store_grad(QP, g, dot(self.an[layer], rows, 1, 1))

        loop(3, body, 3)

    def pair_grad(self, p):
        rows = [self.dqkv[g * D + p * PAIR : g * D + (p + 1) * PAIR, :] for g in range(3)]
        value = dot(self.an[0], jnp.concatenate(rows, axis=0), 1, 1).astype(bf16)
        value = value.reshape(self.Z, CORES, self.UR, 3 * PAIR)
        for g in range(3):
            part = value[:, :, :, g * PAIR : (g + 1) * PAIR]
            self.gb[QP, g // 2, g % 2, :, :, :, p * PAIR : (p + 1) * PAIR] = part

    def qkv_back(self, layer):
        slot = 2 * layer

        def body(at):
            grad = dot(self.w_qkv(layer), self.dqkv[:, at], 1, 0)
            total = self.dy[:, at] + self.norm_back(grad, slot, at)
            self.dy[:, at] = total
            if layer == 0:
                self.cots[at, :] = total.astype(bf16).T

        self.chunks(body)


    def gain_slots(self):
        mine = self.gslot.at[self.z]
        return [self.remote(mine, mine, self.ns.at[0], self.nr.at[0], p) for p in self.z_peers]

    def gain_stages(self):
        stages = [[self.core_peer], self.group_peers, self.z_peers]
        return stages + [self.r_peers] if self.R > 1 else stages

    def swap_gains(self, stage):
        stages = self.gain_stages()
        at = sum(len(peers) for peers in stages[:stage])
        return [
            self.remote(
                self.nsum.at[stage], self.nin.at[at + k],
                self.ns.at[1 + stage], self.nr.at[1 + stage], peer,
            )
            for k, peer in enumerate(stages[stage])
        ]

    def fold_gains(self, stage):
        stages = self.gain_stages()
        at = sum(len(peers) for peers in stages[:stage])
        came = self.nin.at[at : at + len(stages[stage])]
        self.settle(came, self.ns.at[1 + stage])
        self.settle(came, self.nr.at[1 + stage])
        total = self.nsum[stage]
        for k in range(len(stages[stage])):
            total = total + self.nin[at + k]
        self.nsum[stage + 1] = total
        if stage + 1 < len(stages):
            self.each(self.swap_gains(stage + 1), "start")


    def run(self):
        Z = self.Z
        loads = [
            pltpu.make_async_copy(src, dst, self.in_sem.at[i])
            for i, (src, dst) in enumerate(
                [(self.tokens, self.toks), (self.cotangent, self.cots)]
                + [
                    pair
                    for layer in range(LAYERS)
                    for pair in (
                        (self.qkv_w.at[layer, self.c], self.sq),
                        (self.proj_w.at[layer, self.c], self.sp),
                        (self.up_w.at[layer, self.c], self.su),
                        (self.down_w.at[layer, :, self.c], self.sd),
                    )
                ]
            )
        ]
        for i in (2, 3, 0, 4, 5, 1):
            loads[i].start()
        self.gslot[...] = jnp.zeros_like(self.gslot)
        for layer in range(LAYERS):
            rounded = self.gains[layer].astype(bf16).astype(f32)
            self.gslot[self.z, 2 * layer : 2 * layer + 2, 0 : D // Z] = rounded
        barrier = pltpu.get_barrier_semaphore()
        peers = [self.core_peer] + self.group_peers + self.z_peers + self.r_peers
        for peer in peers:
            pl.semaphore_signal(barrier, inc=1, device_id=peer, device_id_type=MESH)
        self.gacc[...] = jnp.zeros_like(self.gacc)

        def take_weights(m):
            layer, kind = divmod(m, 3)
            at = 2 + 4 * layer
            parts = [at, at + 1] if kind == QP else [at + 1 + kind]
            for i in parts:
                loads[i].wait()
            if kind == QP:
                self.wqp[layer, self.z, self.c, :, 0 : 3 * D] = self.sq[...].astype(bf16)
                self.wqp[layer, self.z, self.c, :, 3 * D : 4 * D] = self.sp[...].astype(bf16)
            elif kind == UP:
                self.wup[layer, self.z, self.c] = self.su[...].astype(bf16)
            else:
                self.wdn[layer, self.z, :, self.c] = self.sd[...].astype(bf16)
            if layer + 1 < LAYERS:
                for i in parts:
                    loads[i + 4].start()

        take_weights(0)
        pl.semaphore_wait(barrier, len(peers))
        self.start_z(0)
        self.each(self.gain_slots(), "start")
        loads[0].wait()

        def take(at):
            self.xs[0, :, at] = self.toks[at, :].T.astype(f32)

        self.chunks(take)
        take_weights(1)
        self.start_g(0)
        self.start_z(1)
        take_weights(2)
        self.start_z(2)
        self.settle(self.gslot.at[0 : Z - 1], self.nr.at[0])
        self.settle(self.gslot.at[0 : Z - 1], self.ns.at[0])
        for z in range(Z):
            tall = jnp.concatenate([self.gslot[z]] * 16, axis=0).T
            for i in range(2 * LAYERS):
                self.gcol[i, z * (D // Z) : (z + 1) * (D // Z), :] = jnp.broadcast_to(
                    tall[0 : D // Z, i : i + 1], (D // Z, 128)
                ).astype(bf16)
        self.first_norm(0)
        self.start_c(0)
        self.make_bias()
        for m in range(3, 3 * LAYERS):
            take_weights(m)
        self.start_g(1)
        self.start_z(3)
        self.ready(0)
        self.project_in(0)
        self.start_g(2)
        self.start_z(4)
        self.start_z(5)

        def heads(body, layer, n, hooks):
            def step(i):
                body(layer, [n * i + a for a in range(n)])
                for at, hook in hooks:
                    pl.when(i == at)(hook)

            loop(HEADS // n, step)

        def do(f, *args):
            return lambda: f(*args)

        heads(self.attend, 0, 3, [(0, do(self.start_g, 3)), (1, do(self.start_c, 1))])
        self.start_g(4)
        self.ready(1)
        self.middle(0)
        self.start_c(2)
        self.start_g(5)
        self.ready(2)
        self.feed(0)
        self.start_c(3)
        self.first_norm(1)
        self.ready(3)
        self.project_in(1)
        heads(self.attend, 1, 3, [(0, do(self.start_c, 4)), (1, do(self.start_c, 5))])
        self.ready(4)
        self.middle(1)
        self.ready(5)
        self.feed(1)
        out_copy = pltpu.make_async_copy(self.toks, self.block_out, self.out_sem.at[0])
        out_copy.start()
        self.gather_sent()

        loads[1].wait()
        valid = self.valid[0]

        def start_back(at):
            where = at.start + lax.broadcasted_iota(jnp.int32, (D, CHUNK), 1)
            grad = self.cots[at, :].T.astype(f32)
            self.dy[:, at] = jnp.where(where < valid, grad, f32(0.0))

        self.chunks(start_back)

        self.feed_back(1)
        self.down_grad(1)
        self.grads_a(D1)
        self.up_grad(1)
        self.grads_a(U1)
        self.grads_b1(D1)
        self.proj_grad(1)
        heads(
            self.attend_back, 1, 2,
            [
                (0, do(self.grads_b1, U1)),
                (1, do(self.grads_b2, D1)),
                (2, do(self.grads_b2, U1)),
            ],
        )
        self.qkv_grad(1)
        self.grads_c(D1)
        self.grads_a(Q1)
        self.qkv_back(1)
        self.grads_c(U1)
        self.grads_b1(Q1)

        self.feed_back(0)
        self.grads_d(D1)
        self.down_grad(0)
        self.grads_a(D0)
        self.grads_b2(Q1)
        self.grads_d(U1)
        self.up_grad(0)
        self.grads_a(U0)
        self.grads_b1(D0)
        self.grads_e(D1)

        def grad_of_pair(p):
            if p == 0:
                self.grads_c(Q1)
                self.proj_grad(0)
            self.pair_grad(p)
            self.grads_a(P0 + p)

        heads(
            self.attend_back, 0, 2,
            [
                (0, do(self.grads_b1, U0)),
                (0, do(grad_of_pair, 0)),
                (0, do(self.grads_e, U1)),
                (1, do(grad_of_pair, 1)),
                (1, do(self.grads_b2, D0)),
                (1, do(self.grads_b1, P0)),
                (1, do(self.grads_f, D1)),
                (2, do(grad_of_pair, 2)),
                (2, do(self.grads_b2, U0)),
                (2, do(self.grads_c, D0)),
                (2, do(self.grads_b, P2)),
                (2, do(self.grads_b1, P1)),
                (2, do(self.grads_b2, P0)),
                (2, do(self.grads_d, Q1)),
                (2, do(self.grads_f, U1)),
            ],
        )
        self.qkv_back(0)
        grad_copy = pltpu.make_async_copy(self.cots, self.tokens_grad, self.out_sem.at[1])
        grad_copy.start()

        lane = lax.broadcasted_iota(jnp.int32, (D, 128), 1)
        tall = jnp.zeros((D, 128), f32)
        for i in range(2 * LAYERS):
            column = jnp.sum(self.gacc[i], axis=1, keepdims=True)
            tall = tall + jnp.where(lane == i, column, f32(0.0))
        self.nsum[0] = tall.T[0:8]
        self.each(self.swap_gains(0), "start")
        self.grads_c(U0)
        self.fold_gains(0)
        self.grads_b2(P1)
        self.grads_c(P2)
        self.grads_c(P0)
        self.grads_d(D0)
        self.grads_e(Q1)
        self.fold_gains(1)
        self.grads_d(P2)
        self.grads_c(P1)
        self.grads_d(P0)
        self.grads_d(U0)
        self.grads_e(D0)
        self.grads_f(Q1)
        self.grads_d(P1)
        self.fold_gains(2)
        if self.R > 1:
            self.fold_gains(3)
        tall = jnp.concatenate([self.nsum[len(self.gain_stages())]] * 16, axis=0).T
        self.gacc[0] = tall
        width = D // Z
        mine = self.gacc[0, pl.ds(pl.multiple_of(self.z * width, 8), width), :]
        mine = jnp.concatenate([mine, jnp.zeros((128 - width, 128), f32)], axis=0).T
        self.gains_grad[...] = mine[0:8]
        self.grads_f(D0)
        self.grads_e(P2)
        self.grads_e(P0)
        self.grads_e(U0)
        self.grads_e(P1)
        self.grads_f(U0)
        for i in (P2, P0, P1):
            self.grads_f(i)
        self.store(0, QP).start()
        out_copy.wait()
        grad_copy.wait()
        for layer in range(LAYERS):
            for t in range(3):
                self.store(layer, t).wait()


def adam(weight, first, second, grad, rate, decay):
    first_new = BETA_ONE * first + (1.0 - BETA_ONE) * grad
    second_new = BETA_TWO * second + (1.0 - BETA_TWO) * grad * grad
    first_fix = 1.0 / (1.0 - BETA_ONE**STEP_COUNT)
    second_fix = 1.0 / (1.0 - BETA_TWO**STEP_COUNT)
    update = first_new * (rate * first_fix) / (jnp.sqrt(second_new * second_fix) + EPS_ADAM)
    return first_new, second_new, weight * (1.0 - rate * decay) - update


def adam_kernel(*refs):
    (block_in, tgrad_in, grads, gains_grad) = refs[:4]
    masters = refs[4:19]
    block_out, tgrad_out = refs[19:21]
    outs = refs[21:]
    rates = (
        2.5 / math.sqrt(D),
        2.5 / math.sqrt(max(4 * D // SEQ, 1)),
        2.5 / math.sqrt(D),
        2.5 / math.sqrt(FF),
        0.5,
    )
    block_out[...] = block_in[...]
    tgrad_out[...] = tgrad_in[...]

    def update(kind, index, grad):
        weight, first, second = (masters[3 * kind + j] for j in range(3))
        new = adam(
            weight[index], first[index], second[index], grad, rates[kind],
            0.1 if kind < 4 else 0.0,
        )
        for j in range(3):
            outs[3 * kind + j][index] = new[j]

    for g in range(GROUPS):
        grad = grads[0, QP, g, 0].astype(f32)
        if g < 3:
            update(0, (0, 0, slice(None), slice(g * D, (g + 1) * D)), grad)
        else:
            update(1, (0, 0), grad)
        update(2, (0, 0, slice(None), slice(g * D, (g + 1) * D)), grads[0, UP, g, 0].astype(f32))
        update(3, (0, g, 0), grads[0, DOWN, g, 0].astype(f32))
    width = masters[12].shape[-1]
    for layer in range(LAYERS):
        update(4, (layer,), gains_grad[2 * layer : 2 * layer + 2, 0:width])


def make_per_device(n_dp, n_fsdp):
    Z, R = n_fsdp, n_dp // UNITS
    UR = D // Z // CORES

    def per_device(
        tokens, cotangent, prefix_len, valid_len,
        qkv_weight, qkv_first, qkv_second,
        proj_weight, proj_first, proj_second,
        up_weight, up_first, up_second,
        down_weight, down_first, down_second,
        norm_gains, gains_first, gains_second,
    ):
        T = tokens.shape[0]
        assert prefix_len.shape == (1,) and T == 4 * BLOCK
        assert Z == 4 and FF // Z // UNITS == UR
        rows4 = lambda w: w.reshape(LAYERS, CORES, UR, w.shape[-1])
        rows5 = lambda w: w.reshape(LAYERS, GROUPS, CORES, UR, D)
        vmem = pltpu.VMEM
        scratch = dict(
            wqp=vmem((LAYERS, Z, CORES, UR, 4 * D), bf16),
            wup=vmem((LAYERS, Z, CORES, UR, FF), bf16),
            wdn=vmem((LAYERS, Z, GROUPS, CORES, UR, D), bf16),
            sq=vmem((UR, 3 * D), f32),
            sp=vmem((UR, D), f32),
            su=vmem((UR, FF), f32),
            sd=vmem((GROUPS, UR, D), f32),
            gslot=vmem((Z, 8, 128), f32),
            gcol=vmem((2 * LAYERS, D, 128), bf16),
            gacc=vmem((2 * LAYERS, D, 128), f32),
            xs=vmem((2 * LAYERS, D, T), f32),
            dy=vmem((D, T), f32),
            an=vmem((LAYERS, D, T), bf16),
            bn=vmem((LAYERS, D, T), bf16),
            qkv=vmem((LAYERS, 3 * D, T), bf16),
            om=vmem((LAYERS, D, T), bf16),
            hid=vmem((LAYERS, FF, T), bf16),
            slope=vmem((LAYERS, FF, T), bf16),
            dqkv=vmem((3 * D, T), bf16),
            dmix=vmem((D, T), bf16),
            dm=vmem((D, T), bf16),
            datt=vmem((D, T), bf16),
            lse=vmem((LAYERS, 8, T), f32),
            stats=vmem((4 * LAYERS, T), f32),
            bias=vmem((5, BLOCK, BLOCK), f32),
            toks=vmem((T, D), bf16),
            cots=vmem((T, D), bf16),
            gb=vmem((3, 2, 2, Z, CORES, UR, D), bf16),
            ra=vmem((4, 2, 2, Z, UR, D), bf16),
            rb1=vmem((4, 2, 2, Z // 2, UR, D), bf16),
            rb2=vmem((4, 2, Z // 2, UR, D), bf16),
            rb=vmem((GROUPS - 1, Z, UR, PAIR), bf16),
            sc=vmem((4, Z, UR, D), bf16),
            rc=vmem((LAYERS, 3, Z - 1, UR, D), bf16),
            fin=vmem((LAYERS, 3, GROUPS, CORES, UR, D), bf16),
            nsum=vmem((5, 8, D), f32),
            nin=vmem((GROUPS + Z + R - 2, 8, D), f32),
        )
        sem = pltpu.SemaphoreType.DMA
        scratch.update(
            zs=sem((1,)),
            zr=sem((Z - 2 + 3 * LAYERS,)),
            gs=sem((3 * LAYERS,)),
            gr=sem((3 * LAYERS, Z - 1)),
            cs=sem((LAYERS,)),
            cr=sem((3 * LAYERS,)),
            rs=sem((len(ITEMS), 6)),
            rr=sem((len(ITEMS), 6)),
            ns=sem((5,)),
            nr=sem((5,)),
            in_sem=sem((2 + 4 * LAYERS,)),
            out_sem=sem((2 + 3 * LAYERS,)),
        )
        if R > 1:
            scratch.update(
                rx=vmem((LAYERS, 3, R - 1, UR, D), bf16),
                rx_out=vmem((LAYERS, 3, UR, D), bf16),
                rxs=sem((len(ITEMS),)),
                rxr=sem((len(ITEMS),)),
            )
        ins = dict(
            tokens=tokens, cotangent=cotangent, prefix=prefix_len, valid=valid_len,
            qkv_w=rows4(qkv_weight), proj_w=rows4(proj_weight), up_w=rows4(up_weight),
            down_w=rows5(down_weight), gains=norm_gains,
        )
        outs = dict(
            block_out=jax.ShapeDtypeStruct((T, D), bf16),
            tokens_grad=jax.ShapeDtypeStruct((T, D), bf16),
            grads_out=jax.ShapeDtypeStruct((LAYERS, 3, GROUPS, CORES, UR, D), bf16),
            gains_grad=jax.ShapeDtypeStruct((8, 128), f32),
        )
        names = list(ins) + list(outs) + list(scratch)
        hbm = pl.BlockSpec(memory_space=pl.ANY)
        smem = pl.BlockSpec(memory_space=pltpu.SMEM)
        local = pl.BlockSpec(memory_space=pltpu.VMEM)

        def kernel(*refs):
            Step(dict(T=T, Z=Z, R=R, UR=UR), dict(zip(names, refs))).run()

        block_mid, tgrad_mid, grads, gains_grad = pl.pallas_call(
            kernel,
            out_shape=list(outs.values()),
            in_specs=[hbm, hbm, smem, smem, hbm, hbm, hbm, hbm, local],
            out_specs=[hbm, hbm, hbm, local],
            scratch_shapes=list(scratch.values()),
            compiler_params=pltpu.CompilerParams(
                collective_id=0, has_side_effects=True, vmem_limit_bytes=63 * 1024 * 1024
            ),
            name="train_step",
        )(*ins.values())

        masters = [
            f(w)
            for f, group in (
                (rows4, (qkv_weight, qkv_first, qkv_second)),
                (rows4, (proj_weight, proj_first, proj_second)),
                (rows4, (up_weight, up_first, up_second)),
                (rows5, (down_weight, down_first, down_second)),
                (lambda w: w, (norm_gains, gains_first, gains_second)),
            )
            for w in group
        ]
        tok_block = pl.BlockSpec((T // 4, D), lambda l, c: (2 * l + c, 0))

        def spec(w):
            if w.ndim == 4:
                return pl.BlockSpec((1, 1, *w.shape[2:]), lambda l, c: (l, c, 0, 0))
            if w.ndim == 5:
                return pl.BlockSpec((1, GROUPS, 1, UR, D), lambda l, c: (l, 0, c, 0, 0))
            return pl.BlockSpec(w.shape, lambda l, c: (0, 0, 0))

        specs = [spec(w) for w in masters]
        done = pl.pallas_call(
            adam_kernel,
            grid=(LAYERS, CORES),
            out_shape=[jax.ShapeDtypeStruct((T, D), bf16)] * 2
            + [jax.ShapeDtypeStruct(w.shape, f32) for w in masters],
            in_specs=[
                tok_block,
                tok_block,
                pl.BlockSpec((1, 3, GROUPS, 1, UR, D), lambda l, c: (l, 0, 0, c, 0, 0)),
                pl.BlockSpec((8, 128), lambda l, c: (0, 0)),
                *specs,
            ],
            out_specs=[tok_block, tok_block, *specs],
            compiler_params=pltpu.CompilerParams(vmem_limit_bytes=62 * 1024 * 1024),
            name="adam",
        )(block_mid, tgrad_mid, grads, gains_grad, *masters)
        shapes = [
            w.shape
            for w in (
                qkv_weight, qkv_first, qkv_second, proj_weight, proj_first, proj_second,
                up_weight, up_first, up_second, down_weight, down_first, down_second,
                norm_gains, gains_first, gains_second,
            )
        ]
        news = [x.reshape(s) for x, s in zip(done[2:], shapes)]
        results = []
        for kind in range(5):
            weight_new, second_new, first_new = news[3 * kind + 2], news[3 * kind + 1], news[3 * kind]
            results += [first_new, second_new, weight_new]
        return (done[0], done[1], *results)

    return per_device


def solution(mesh):
    rows = P(("dp", "fsdp"), None)
    lens = P(("dp", "fsdp"))
    weight = P(None, "fsdp", None)
    gain = P(None, None, "fsdp")
    return jax.shard_map(
        make_per_device(mesh.shape["dp"], mesh.shape["fsdp"]),
        mesh=mesh,
        in_specs=(rows, rows, lens, lens, *([weight] * 12), *([gain] * 3)),
        out_specs=(rows, rows, *([weight] * 12), *([gain] * 3)),
        check_vma=False,
    )
```

```python
import functools
import math

import jax
import jax.numpy as jnp
from jax import lax
from jax.experimental import pallas as pl
from jax.experimental.pallas import tpu as pltpu
from jax.sharding import PartitionSpec as P

D = 384
HEADS = 6
HEAD_DIM = 64
FF = 1536
SEQ = 1024
STEP_COUNT = 7

NEG_FILL = -1e30
EPS_NORM = 1e-05
EPS_ADAM = 1e-08
BETA_ONE = 0.9
BETA_TWO = 0.99

LAYERS = 2
GROUPS = 4
CORES = 2
UNITS = GROUPS * CORES
BLOCK = 256
CHUNK = 512
QP, UP, DOWN = 0, 1, 2
PAIR = 2 * HEAD_DIM
ITEMS = [(layer, kind, kind, pl.ds(0, D)) for layer, kind in ((1, DOWN), (1, UP), (1, QP), (0, DOWN), (0, UP))]
ITEMS += [(0, QP, 3, pl.ds(p * PAIR, PAIR)) for p in range(3)]
D1, U1, Q1, D0, U0, P0, P1, P2 = range(8)
LAST = P2

MESH = pl.DeviceIdType.MESH
bf16 = jnp.bfloat16
f32 = jnp.float32


def dot(left, right, left_dim, right_dim):
    return lax.dot_general(
        left, right, (((left_dim,), (right_dim,)), ((), ())), preferred_element_type=f32
    )


def loop(count, body, unroll=1):
    def step(index, carry):
        body(index)
        return carry

    lax.fori_loop(0, count, step, 0, unroll=unroll)


class Remote:
    def __init__(self, src, dst, send, recv, device):
        self.made = lambda: pltpu.make_async_remote_copy(
            src_ref=src, dst_ref=dst, send_sem=send, recv_sem=recv,
            device_id=device, device_id_type=MESH,
        )

    def start(self):
        self.made().start()

    def wait_send(self):
        self.made().wait_send()

    def wait_recv(self):
        self.made().wait_recv()

    def wait(self):
        self.made().wait()


class Step:
    def __init__(self, sizes, refs):
        self.__dict__.update(sizes)
        self.__dict__.update(refs)
        self.dp = lax.axis_index("dp")
        self.z = lax.axis_index("fsdp")
        self.unit = self.dp % UNITS
        self.c = self.unit % CORES
        self.g = self.unit // CORES
        self.base = self.dp - self.unit
        self.core_peer = (self.base + self.g * CORES + (1 - self.c), self.z)
        gx, gy = self.g % 2, self.g // 2
        self.gx, self.gy = gx, gy
        self.others = [gy * 2 + (1 - gx), (1 - gy) * 2 + gx, (1 - gy) * 2 + (1 - gx)]
        self.group_peers = [(self.base + g * CORES + self.c, self.z) for g in self.others]
        self.z_others = []
        for k in range(1, self.Z):
            other, bit = 0, 1
            while bit < self.Z:
                own = (self.z // bit) % 2
                other = other + bit * (1 - own if k & bit else own)
                bit *= 2
            self.z_others.append(other)
        self.z_peers = [(self.dp, z) for z in self.z_others]
        total = self.R * UNITS
        self.r_peers = [((self.dp + j * UNITS) % total, self.z) for j in range(1, self.R)]


    def remote(self, src, dst, send, recv, device):
        return Remote(src, dst, send, recv, device)

    def weight_unit(self, kind, layer, z, g, c):
        if kind == DOWN:
            return self.wdn.at[layer, z, g, c]
        whole = self.wqp if kind == QP else self.wup
        return whole.at[layer, z, c, :, pl.ds(pl.multiple_of(g * D, 128), D)]

    def weight_half(self, kind, layer, z, c):
        if kind == DOWN:
            return self.wdn.at[layer, z, :, c]
        return (self.wqp if kind == QP else self.wup).at[layer, z, c]

    def settle(self, ref, sem):
        pltpu.make_async_copy(ref, ref, sem).wait()

    def gather_z(self, m):
        layer, kind = divmod(m, 3)
        mine = self.weight_unit(kind, layer, self.z, self.g, self.c)
        arrived = [self.zr.at[k if m == 0 else self.Z - 2 + m] for k in range(self.Z - 1)]
        return [
            self.remote(mine, mine, self.zs.at[0], arrived[k], peer)
            for k, peer in enumerate(self.z_peers)
        ]

    def gather_g(self, m, k):
        layer, kind = divmod(m, 3)
        mine = self.weight_unit(kind, layer, self.z_others[k], self.g, self.c)
        return [
            self.remote(mine, mine, self.gs.at[m], self.gr.at[m, k], peer)
            for peer in self.group_peers
        ]

    def gather_c(self, m, k):
        layer, kind = divmod(m, 3)
        z = self.z if k == self.Z - 1 else self.z_others[k]
        mine = self.weight_half(kind, layer, z, self.c)
        return self.remote(mine, mine, self.cs.at[layer], self.cr.at[m], self.core_peer)

    def start_z(self, m):
        self.each(self.gather_z(m), "start")
        self.gather_c(m, self.Z - 1).start()

    def start_g(self, m):
        if m > 0:
            self.settle(self.rc.at[0, 0], self.zr.at[self.Z - 2 + m])
        for k in range(self.Z - 1):
            if m == 0:
                self.settle(self.rc.at[0, 0, 0], self.zr.at[k])
            self.each(self.gather_g(m, k), "start")
            if m == 0 and k < 2:
                self.start_z(1 + k)

    def start_c(self, m):
        for k in range(self.Z - 1):
            self.settle(self.rc.at[0, 0], self.gr.at[m, k])
            self.gather_c(m, k).start()

    def ready(self, m):
        self.settle(self.fin.at[0, 0:2], self.cr.at[m])

    def gather_sent(self):
        self.settle(self.fin.at[0, :, 0:3], self.zs.at[0])
        for m in range(3 * LAYERS):
            self.settle(self.rc.at[0], self.gs.at[m])
        for layer in range(LAYERS):
            self.settle(self.fin, self.cs.at[layer])


    def reduce_a(self, i):
        layer, t, buf, cols = ITEMS[i]
        return self.remote(
            self.gb.at[t, :, :, :, 1 - self.c, :, cols], self.ra.at[buf, :, :, :, :, cols],
            self.rs.at[i, 0], self.rr.at[i, 0], self.core_peer,
        )

    def reduce_b1(self, i):
        layer, t, buf, cols = ITEMS[i]
        half = self.Z // 2
        return [
            self.remote(
                self.gb.at[t, :, 1 - self.gx, 0:half, self.c, :, cols],
                self.rb1.at[buf, 0, :, :, :, cols],
                self.rs.at[i, 1], self.rr.at[i, 1], self.group_peers[0],
            ),
            self.remote(
                self.gb.at[t, 1 - self.gy, :, half:, self.c, :, cols],
                self.rb1.at[buf, 1, :, :, :, cols],
                self.rs.at[i, 1], self.rr.at[i, 1], self.group_peers[1],
            ),
        ]

    def reduce_b2(self, i):
        layer, t, buf, cols = ITEMS[i]
        half = self.Z // 2
        return [
            self.remote(
                self.gb.at[t, 1 - self.gy, self.gx, 0:half, self.c, :, cols],
                self.rb2.at[buf, 0, :, :, cols],
                self.rs.at[i, 2], self.rr.at[i, 2], self.group_peers[1],
            ),
            self.remote(
                self.gb.at[t, self.gy, 1 - self.gx, half:, self.c, :, cols],
                self.rb2.at[buf, 1, :, :, cols],
                self.rs.at[i, 2], self.rr.at[i, 2], self.group_peers[0],
            ),
        ]

    def reduce_b(self, i):
        layer, t, buf, cols = ITEMS[i]
        return [
            self.remote(
                self.gb.at[t, self.others[k] // 2, self.others[k] % 2, :, self.c, :, cols],
                self.rb.at[k],
                self.rs.at[i, 1], self.rr.at[i, 1], peer,
            )
            for k, peer in enumerate(self.group_peers)
        ]

    def reduce_c(self, i):
        layer, t, buf, cols = ITEMS[i]
        return [
            self.remote(
                self.sc.at[buf, self.z_others[k], :, cols], self.rc.at[layer, t, k, :, cols],
                self.rs.at[i, 3], self.rr.at[i, 3], peer,
            )
            for k, peer in enumerate(self.z_peers)
        ]

    def reduce_r(self, i):
        layer, t, buf, cols = ITEMS[i]
        return [
            self.remote(
                self.rx_out.at[layer, t, :, cols], self.rx.at[layer, t, j, :, cols],
                self.rxs.at[i], self.rxr.at[i], peer,
            )
            for j, peer in enumerate(self.r_peers)
        ]

    def reduce_d(self, i):
        layer, t, buf, cols = ITEMS[i]
        mine = self.fin.at[layer, t, self.g, self.c, :, cols]
        return [
            self.remote(mine, mine, self.rs.at[i, 4], self.rr.at[i, 4], peer)
            for peer in self.group_peers
        ]

    def reduce_e(self, i):
        layer, t, buf, cols = ITEMS[i]
        mine = self.fin.at[layer, t, :, self.c, :, cols]
        return self.remote(mine, mine, self.rs.at[i, 5], self.rr.at[i, 5], self.core_peer)

    def settle_both(self, ref, i, stage):
        self.settle(ref, self.rs.at[i, stage])
        self.settle(ref, self.rr.at[i, stage])

    def each(self, copies, action):
        for copy in copies:
            getattr(copy, action)()

    def grads_a(self, i):
        self.reduce_a(i).start()

    def add_cores(self, i):
        layer, t, buf, cols = ITEMS[i]
        self.settle_both(self.ra.at[buf, :, :, :, :, cols], i, 0)

        def add(g):
            at = (t, g // 2, g % 2, slice(None), self.c, slice(None), cols)
            both = self.gb[at].astype(f32) + self.ra[buf, g // 2, g % 2, :, :, cols].astype(f32)
            self.gb[at] = both.astype(bf16)

        loop(GROUPS, add)

    def grads_b1(self, i):
        self.add_cores(i)
        self.each(self.reduce_b1(i), "start")

    def grads_b2(self, i):
        layer, t, buf, cols = ITEMS[i]
        half = self.Z // 2
        self.settle_both(self.rb1.at[buf, :, :, :, :, cols], i, 1)
        at = (t, slice(None), self.gx, slice(0, half), self.c, slice(None), cols)
        both = self.gb[at].astype(f32) + self.rb1[buf, 0, :, :, :, cols].astype(f32)
        self.gb[at] = both.astype(bf16)
        at = (t, self.gy, slice(None), slice(half, self.Z), self.c, slice(None), cols)
        both = self.gb[at].astype(f32) + self.rb1[buf, 1, :, :, :, cols].astype(f32)
        self.gb[at] = both.astype(bf16)
        self.each(self.reduce_b2(i), "start")

    def grads_b(self, i):
        self.add_cores(i)
        self.each(self.reduce_b(i), "start")

    def grads_c(self, i):
        layer, t, buf, cols = ITEMS[i]
        half = self.Z // 2
        if i == LAST:
            self.settle_both(self.rb, i, 1)
            total = self.gb[t, self.gy, self.gx, :, self.c, :, cols].astype(f32)
            for k in range(GROUPS - 1):
                total = total + self.rb[k].astype(f32)
            self.sc[buf, :, :, cols] = total.astype(bf16)
        else:
            self.settle_both(self.rb2.at[buf, :, :, :, cols], i, 2)
            for j in range(2):
                span = slice(j * half, (j + 1) * half)
                total = self.gb[t, self.gy, self.gx, span, self.c, :, cols].astype(f32)
                total = total + self.rb2[buf, j, :, :, cols].astype(f32)
                self.sc[buf, span, :, cols] = total.astype(bf16)
        self.each(self.reduce_c(i), "start")

    def grads_d(self, i):
        layer, t, buf, cols = ITEMS[i]
        self.settle_both(self.rc.at[layer, t, :, :, cols], i, 3)
        total = self.sc[buf, self.z, :, cols].astype(f32)
        for k in range(self.Z - 1):
            total = total + self.rc[layer, t, k, :, cols].astype(f32)
        if self.R > 1:
            self.rx_out[layer, t, :, cols] = total.astype(bf16)
            self.each(self.reduce_r(i), "start")
            self.settle(self.rx.at[layer, t, :, :, cols], self.rxs.at[i])
            self.settle(self.rx.at[layer, t, :, :, cols], self.rxr.at[i])
            for j in range(self.R - 1):
                total = total + self.rx[layer, t, j, :, cols].astype(f32)
        self.fin[layer, t, self.g, self.c, :, cols] = total.astype(bf16)
        self.each(self.reduce_d(i), "start")

    def grads_e(self, i):
        layer, t, buf, cols = ITEMS[i]
        self.settle_both(self.rc.at[layer, t, :, :, cols], i, 4)
        self.reduce_e(i).start()

    def grads_f(self, i):
        layer, t, buf, cols = ITEMS[i]
        self.settle_both(self.fin.at[layer, t, :, 1 - self.c, :, cols], i, 5)
        if buf < 3:
            self.store(layer, t).start()

    def store(self, layer, t):
        return pltpu.make_async_copy(
            self.fin.at[layer, t], self.grads_out.at[layer, t], self.out_sem.at[2 + 3 * layer + t]
        )


    def chunks(self, body, unroll=1):
        loop(self.T // CHUNK, lambda i: body(pl.ds(pl.multiple_of(i * CHUNK, CHUNK), CHUNK)), unroll)

    def spread(self, index):
        column = self.gcol[index].astype(f32)
        return jnp.concatenate([column] * (CHUNK // 128), axis=1)

    def normed(self, x, slot, at):
        mean = jnp.sum(x, axis=0, keepdims=True) * (1.0 / D)
        centered = x - mean
        inverse = lax.rsqrt(
            jnp.sum(centered * centered, axis=0, keepdims=True) * (1.0 / D) + EPS_NORM
        )
        self.stats[2 * slot : 2 * slot + 1, at] = mean
        self.stats[2 * slot + 1 : 2 * slot + 2, at] = inverse
        return centered * inverse

    def norm_back(self, grad, slot, at):
        mean = self.stats[2 * slot : 2 * slot + 1, at]
        inverse = self.stats[2 * slot + 1 : 2 * slot + 2, at]
        normed = (self.xs[slot, :, at] - mean) * inverse
        product = grad * normed
        partial = product[:, 0:128]
        for j in range(1, CHUNK // 128):
            partial = partial + product[:, j * 128 : (j + 1) * 128]
        self.gacc[slot] += partial
        gain = self.spread(slot)
        scaled = grad * gain
        average = jnp.sum(scaled, axis=0, keepdims=True) * (1.0 / D)
        along = jnp.sum(product * gain, axis=0, keepdims=True) * (1.0 / D)
        return inverse * (scaled - average - normed * along)

    def w_qkv(self, layer):
        return self.wqp[layer, :, :, :, 0 : 3 * D].reshape(D, 3 * D)

    def w_proj(self, layer):
        return self.wqp[layer, :, :, :, 3 * D : 4 * D].reshape(D, D)

    def w_up(self, layer):
        return self.wup[layer].reshape(D, FF)

    def w_down(self, layer):
        return self.wdn[layer].reshape(FF, D)

    def make_bias(self):
        prefix, valid = self.prefix[0], self.valid[0]
        key = lax.broadcasted_iota(jnp.int32, (BLOCK, BLOCK), 0)
        query = lax.broadcasted_iota(jnp.int32, (BLOCK, BLOCK), 1)
        causal = key <= query
        fill = lambda ok: jnp.where(ok, f32(0.0), f32(NEG_FILL))
        self.bias[0] = fill(causal | (key < prefix))
        self.bias[1] = fill(causal)
        self.bias[2] = fill(causal & (key + 2 * BLOCK < valid))
        self.bias[3] = fill(causal & (key + 3 * BLOCK < valid))
        self.bias[4] = fill(key + 2 * BLOCK < valid)

    def score_blocks(self, keys_t, queries, q):
        blocks = []
        for j in range(q + 1):
            s = dot(keys_t[j * BLOCK : (j + 1) * BLOCK], queries, 1, 0)
            if j == q:
                s = s + self.bias[q]
            elif j == 2:
                s = s + self.bias[4]
            blocks.append(s)
        return blocks

    def head_rows(self, h, part):
        return pl.ds(pl.multiple_of(part * D + h * HEAD_DIM, HEAD_DIM), HEAD_DIM)

    def attend(self, layer, heads):
        count = self.T // BLOCK
        span = lambda q: slice(q * BLOCK, (q + 1) * BLOCK)
        queries = [self.qkv[layer, self.head_rows(h, 0), :] for h in heads]
        keys_t = [self.qkv[layer, self.head_rows(h, 1), :].T for h in heads]
        ones = jnp.ones((16, self.T), bf16)
        values = [
            jnp.concatenate([self.qkv[layer, self.head_rows(h, 2), :], ones], axis=0) for h in heads
        ]

        def scores(a, q):
            return self.score_blocks(keys_t[a], queries[a][:, span(q)], q)

        def soften(blocks):
            largest = functools.reduce(
                jnp.maximum, [jnp.max(s, axis=0, keepdims=True) for s in blocks]
            )
            probs = jnp.concatenate([jnp.exp(s - largest).astype(bf16) for s in blocks], axis=0)
            return largest, probs

        def mix(a, q, largest, probs):
            mixed = dot(values[a][:, : (q + 1) * BLOCK], probs, 1, 0)
            denominator = mixed[HEAD_DIM : HEAD_DIM + 1]
            mixed = mixed[:HEAD_DIM] * (1.0 / denominator)
            self.om[layer, self.head_rows(heads[a], 0), span(q)] = mixed.astype(bf16)
            self.lse[layer, pl.ds(heads[a], 1), span(q)] = largest + jnp.log(denominator)

        self.pipeline(len(heads), range(count), scores, lambda a, q, s: soften(s), mix)

    def pipeline(self, n, order, first, second, third):
        work = [(a, q) for q in order for a in range(n)]
        now = first(*work[0])
        last = None
        for i, place in enumerate(work):
            ahead = first(*work[i + 1]) if i + 1 < len(work) else None
            made = second(*place, now)
            if last is not None:
                third(*last[0], *last[1])
            last, now = (place, made), ahead
        third(*last[0], *last[1])

    def attend_back(self, layer, heads):
        count = self.T // BLOCK
        span = lambda q: slice(q * BLOCK, (q + 1) * BLOCK)
        part = lambda i: [self.qkv[layer, self.head_rows(h, i), :] for h in heads]
        queries, keys, values = part(0), part(1), part(2)
        keys_t, values_t = [k.T for k in keys], [v.T for v in values]
        grads = [self.dmix[self.head_rows(h, 0), :] for h in heads]
        delta = [
            jnp.sum(
                g.astype(f32) * self.om[layer, self.head_rows(h, 0), :].astype(f32),
                axis=0, keepdims=True,
            )
            for g, h in zip(grads, heads)
        ]
        key_grads = [[None] * count for h in heads]
        value_grads = [[None] * count for h in heads]

        def first(a, q):
            scores = self.score_blocks(keys_t[a], queries[a][:, span(q)], q)
            slopes = [dot(values_t[a][span(j)], grads[a][:, span(q)], 1, 0) for j in range(q + 1)]
            return scores, slopes

        def second(a, q, made):
            total = self.lse[layer, pl.ds(heads[a], 1), span(q)]
            low, small = [], []
            for s, slope in zip(*made):
                probs = jnp.exp(s - total)
                low.append(probs.astype(bf16))
                small.append((probs * (slope - delta[a][:, span(q)])).astype(bf16))
            return jnp.concatenate(low, axis=0), jnp.concatenate(small, axis=0)

        def third(a, q, probs, d_scores):
            k_part = dot(queries[a][:, span(q)], d_scores, 1, 1)
            v_part = dot(grads[a][:, span(q)], probs, 1, 1)
            for j in range(q + 1):
                for grad, more in ((key_grads[a], k_part), (value_grads[a], v_part)):
                    grad[j] = more[:, span(j)] if grad[j] is None else grad[j] + more[:, span(j)]
            q_part = dot(keys[a][:, : (q + 1) * BLOCK], d_scores, 1, 0) * (HEAD_DIM**-0.5)
            self.dqkv[self.head_rows(heads[a], 0), span(q)] = q_part.astype(bf16)

        self.pipeline(len(heads), reversed(range(count)), first, second, third)
        for a, h in enumerate(heads):
            self.dqkv[self.head_rows(h, 1), :] = jnp.concatenate(key_grads[a], axis=1).astype(bf16)
            self.dqkv[self.head_rows(h, 2), :] = jnp.concatenate(value_grads[a], axis=1).astype(bf16)

    def first_norm(self, layer):
        slot = 2 * layer

        def body(at):
            n = self.normed(self.xs[slot, :, at], slot, at)
            self.an[layer, :, at] = (n * self.spread(slot)).astype(bf16)

        self.chunks(body)

    def project_in(self, layer):
        def body(at):
            rows = dot(self.w_qkv(layer), self.an[layer, :, at], 0, 0)
            self.qkv[layer, 0:D, at] = (rows[0:D] * (HEAD_DIM**-0.5)).astype(bf16)
            self.qkv[layer, D : 3 * D, at] = rows[D:].astype(bf16)

        self.chunks(body)

    def middle(self, layer):
        slot = 2 * layer + 1

        def body(at):
            x = self.xs[slot - 1, :, at] + dot(self.w_proj(layer), self.om[layer, :, at], 0, 0)
            self.xs[slot, :, at] = x
            n = self.normed(x, slot, at)
            self.bn[layer, :, at] = (n * self.spread(slot)).astype(bf16)

        self.chunks(body)

    def feed_up(self, layer):
        def body(at):
            def first(a, j):
                weight = self.wup[layer, :, :, :, j * D : (j + 1) * D].reshape(D, D)
                return dot(weight, self.bn[layer, :, at], 0, 0)

            def second(a, j, u):
                rows = slice(j * D, (j + 1) * D)
                area = 0.5 + 0.5 * lax.erf(u * (0.5**0.5))
                density = jnp.exp(u * u * (-0.5)) * (1.0 / math.sqrt(2.0 * math.pi))
                self.hid[layer, rows, at] = (u * area).astype(bf16)
                self.slope[layer, rows, at] = (area + u * density).astype(bf16)
                return ()

            self.pipeline(1, range(FF // D), first, second, lambda a, j: None)

        self.chunks(body)

    def feed_down(self, layer):
        def body(at):
            x = self.xs[2 * layer + 1, :, at]
            x = x + dot(self.w_down(layer), self.hid[layer, :, at], 0, 0)
            if layer + 1 < LAYERS:
                self.xs[2 * layer + 2, :, at] = x
            else:
                self.toks[at, :] = x.astype(bf16).T

        self.chunks(body)

    def feed_back(self, layer):
        slot = 2 * layer + 1

        def body(at):
            d_hidden = dot(self.w_down(layer), self.dm[:, at], 1, 0)
            d_pre = (d_hidden * self.slope[layer, :, at].astype(f32)).astype(bf16)
            self.slope[layer, :, at] = d_pre
            grad = dot(self.w_up(layer), d_pre, 1, 0)
            total = self.dy[:, at] + self.norm_back(grad, slot, at)
            self.dy[:, at] = total
            low = total.astype(bf16)
            self.datt[:, at] = low
            self.dmix[:, at] = dot(self.w_proj(layer), low, 1, 0).astype(bf16)

        self.chunks(body)

    def down_grad(self, layer):
        width = FF // self.Z

        def body(z):
            rows = self.hid[layer, pl.ds(pl.multiple_of(z * width, 64), width), :]
            value = dot(rows, self.dm[...], 1, 1).astype(bf16)
            self.gb[DOWN, :, :, z] = value.reshape(2, 2, CORES, self.UR, D)

        loop(self.Z, body, self.Z)

    def store_grad(self, t, g, value):
        self.gb[t, g // 2, g % 2] = value.astype(bf16).reshape(self.Z, CORES, self.UR, D)

    def up_grad(self, layer):
        def body(g):
            rows = self.slope[layer, pl.ds(pl.multiple_of(g * D, 64), D), :]
            self.store_grad(UP, g, dot(self.bn[layer], rows, 1, 1))

        loop(GROUPS, body, GROUPS)

    def proj_grad(self, layer):
        self.store_grad(QP, 3, dot(self.om[layer], self.datt[...], 1, 1))

    def qkv_grad(self, layer):
        def body(g):
            rows = self.dqkv[pl.ds(pl.multiple_of(g * D, 64), D), :]
            self.store_grad(QP, g, dot(self.an[layer], rows, 1, 1))

        loop(3, body, 3)

    def pair_grad(self, p):
        rows = [self.dqkv[g * D + p * PAIR : g * D + (p + 1) * PAIR, :] for g in range(3)]
        value = dot(self.an[0], jnp.concatenate(rows, axis=0), 1, 1).astype(bf16)
        value = value.reshape(self.Z, CORES, self.UR, 3 * PAIR)
        for g in range(3):
            part = value[:, :, :, g * PAIR : (g + 1) * PAIR]
            self.gb[QP, g // 2, g % 2, :, :, :, p * PAIR : (p + 1) * PAIR] = part

    def qkv_back(self, layer):
        slot = 2 * layer

        def body(at):
            grad = dot(self.w_qkv(layer), self.dqkv[:, at], 1, 0)
            total = self.dy[:, at] + self.norm_back(grad, slot, at)
            if layer == 0:
                self.cots[at, :] = total.astype(bf16).T
            else:
                self.dy[:, at] = total
                self.dm[:, at] = total.astype(bf16)

        self.chunks(body)


    def gain_slots(self):
        mine = self.gslot.at[self.z]
        return [self.remote(mine, mine, self.ns.at[0], self.nr.at[0], p) for p in self.z_peers]

    def gain_stages(self):
        stages = [[self.core_peer], self.group_peers, self.z_peers]
        return stages + [self.r_peers] if self.R > 1 else stages

    def swap_gains(self, stage):
        stages = self.gain_stages()
        at = sum(len(peers) for peers in stages[:stage])
        return [
            self.remote(
                self.nsum.at[stage], self.nin.at[at + k],
                self.ns.at[1 + stage], self.nr.at[1 + stage], peer,
            )
            for k, peer in enumerate(stages[stage])
        ]

    def fold_gains(self, stage):
        stages = self.gain_stages()
        at = sum(len(peers) for peers in stages[:stage])
        came = self.nin.at[at : at + len(stages[stage])]
        self.settle(came, self.ns.at[1 + stage])
        self.settle(came, self.nr.at[1 + stage])
        total = self.nsum[stage]
        for k in range(len(stages[stage])):
            total = total + self.nin[at + k]
        self.nsum[stage + 1] = total
        if stage + 1 < len(stages):
            self.each(self.swap_gains(stage + 1), "start")


    def run(self):
        Z = self.Z
        loads = [
            pltpu.make_async_copy(src, dst, self.in_sem.at[i])
            for i, (src, dst) in enumerate(
                [(self.tokens, self.toks), (self.cotangent, self.cots)]
                + [
                    pair
                    for layer in range(LAYERS)
                    for pair in (
                        (self.qkv_w.at[layer, self.c], self.sq),
                        (self.proj_w.at[layer, self.c], self.sp),
                        (self.up_w.at[layer, self.c], self.su),
                        (self.down_w.at[layer, :, self.c], self.sd),
                    )
                ]
            )
        ]
        for i in (2, 3, 0, 4, 5, 1):
            loads[i].start()
        self.gslot[...] = jnp.zeros_like(self.gslot)
        for layer in range(LAYERS):
            rounded = self.gains[layer].astype(bf16).astype(f32)
            self.gslot[self.z, 2 * layer : 2 * layer + 2, 0 : D // Z] = rounded
        barrier = pltpu.get_barrier_semaphore()
        peers = [self.core_peer] + self.group_peers + self.z_peers + self.r_peers
        for peer in peers:
            pl.semaphore_signal(barrier, inc=1, device_id=peer, device_id_type=MESH)
        self.gacc[...] = jnp.zeros_like(self.gacc)

        def take_weights(m):
            layer, kind = divmod(m, 3)
            at = 2 + 4 * layer
            parts = [at, at + 1] if kind == QP else [at + 1 + kind]
            for i in parts:
                loads[i].wait()
            if kind == QP:
                self.wqp[layer, self.z, self.c, :, 0 : 3 * D] = self.sq[...].astype(bf16)
                self.wqp[layer, self.z, self.c, :, 3 * D : 4 * D] = self.sp[...].astype(bf16)
            elif kind == UP:
                self.wup[layer, self.z, self.c] = self.su[...].astype(bf16)
            else:
                self.wdn[layer, self.z, :, self.c] = self.sd[...].astype(bf16)
            if layer + 1 < LAYERS:
                for i in parts:
                    loads[i + 4].start()

        take_weights(0)
        pl.semaphore_wait(barrier, len(peers))
        self.start_z(0)
        self.each(self.gain_slots(), "start")
        loads[0].wait()

        def take(at):
            self.xs[0, :, at] = self.toks[at, :].T.astype(f32)

        take_weights(1)
        take_weights(2)
        self.start_g(0)
        self.chunks(take)
        self.settle(self.gslot.at[0 : Z - 1], self.nr.at[0])
        self.settle(self.gslot.at[0 : Z - 1], self.ns.at[0])
        for z in range(Z):
            tall = jnp.concatenate([self.gslot[z]] * 16, axis=0).T
            for i in range(2 * LAYERS):
                self.gcol[i, z * (D // Z) : (z + 1) * (D // Z), :] = jnp.broadcast_to(
                    tall[0 : D // Z, i : i + 1], (D // Z, 128)
                ).astype(bf16)
        self.first_norm(0)
        self.start_c(0)
        self.make_bias()
        for m in range(3, 3 * LAYERS):
            take_weights(m)
        self.start_g(1)
        self.start_z(3)
        self.ready(0)
        self.project_in(0)
        self.start_g(2)
        self.start_z(4)
        self.start_z(5)

        def heads(body, layer, n, hooks):
            def step(i):
                body(layer, [n * i + a for a in range(n)])
                for at, hook in hooks:
                    pl.when(i == at)(hook)

            loop(HEADS // n, step)

        def do(f, *args):
            return lambda: f(*args)

        heads(self.attend, 0, 3, [(0, do(self.start_g, 3)), (1, do(self.start_c, 1))])
        self.middle(0)
        self.start_g(4)
        self.ready(1)
        self.feed_up(0)
        self.start_c(2)
        self.start_g(5)
        self.ready(2)
        self.feed_down(0)
        self.start_c(3)
        self.first_norm(1)
        self.ready(3)
        self.project_in(1)
        heads(self.attend, 1, 3, [(0, do(self.start_c, 4))])
        self.ready(4)
        self.middle(1)
        self.start_c(5)
        self.feed_up(1)
        self.ready(5)
        self.feed_down(1)
        out_copy = pltpu.make_async_copy(self.toks, self.block_out, self.out_sem.at[0])
        out_copy.start()
        self.gather_sent()

        loads[1].wait()
        valid = self.valid[0]

        def start_back(at):
            where = at.start + lax.broadcasted_iota(jnp.int32, (D, CHUNK), 1)
            grad = self.cots[at, :].T.astype(f32)
            grad = jnp.where(where < valid, grad, f32(0.0))
            self.dy[:, at] = grad
            self.dm[:, at] = grad.astype(bf16)

        self.chunks(start_back)

        self.down_grad(1)
        self.grads_a(D1)
        self.feed_back(1)
        self.grads_b1(D1)
        self.up_grad(1)
        self.grads_a(U1)
        self.proj_grad(1)
        heads(
            self.attend_back, 1, 2,
            [
                (0, do(self.grads_b1, U1)),
                (0, do(self.grads_b2, D1)),
                (2, do(self.grads_b2, U1)),
                (2, do(self.grads_c, D1)),
            ],
        )
        self.qkv_grad(1)
        self.grads_a(Q1)
        self.qkv_back(1)
        self.grads_b1(Q1)
        self.grads_c(U1)

        self.down_grad(0)
        self.grads_a(D0)
        self.grads_d(D1)
        self.feed_back(0)
        self.grads_b2(Q1)
        self.grads_b1(D0)
        self.grads_d(U1)
        self.up_grad(0)
        self.grads_a(U0)
        self.grads_e(D1)

        def grad_of_pair(p):
            if p == 0:
                self.grads_c(Q1)
                self.proj_grad(0)
            self.pair_grad(p)
            self.grads_a(P0 + p)

        heads(
            self.attend_back, 0, 2,
            [
                (0, do(self.grads_b1, U0)),
                (0, do(grad_of_pair, 0)),
                (0, do(self.grads_e, U1)),
                (1, do(grad_of_pair, 1)),
                (1, do(self.grads_b2, D0)),
                (1, do(self.grads_b1, P0)),
                (1, do(self.grads_f, D1)),
                (2, do(grad_of_pair, 2)),
                (2, do(self.grads_b2, U0)),
                (2, do(self.grads_c, D0)),
                (2, do(self.grads_b1, P1)),
                (2, do(self.grads_b2, P0)),
                (2, do(self.grads_d, Q1)),
                (2, do(self.grads_f, U1)),
                (2, do(self.grads_b, P2)),
            ],
        )
        self.qkv_back(0)
        grad_copy = pltpu.make_async_copy(self.cots, self.tokens_grad, self.out_sem.at[1])
        grad_copy.start()

        lane = lax.broadcasted_iota(jnp.int32, (D, 128), 1)
        tall = jnp.zeros((D, 128), f32)
        for i in range(2 * LAYERS):
            column = jnp.sum(self.gacc[i], axis=1, keepdims=True)
            tall = tall + jnp.where(lane == i, column, f32(0.0))
        self.nsum[0] = tall.T[0:8]
        self.each(self.swap_gains(0), "start")
        self.grads_b2(P1)
        self.fold_gains(0)
        self.grads_c(U0)
        self.grads_c(P0)
        self.grads_d(D0)
        self.grads_e(Q1)
        self.grads_c(P2)
        self.grads_c(P1)
        self.fold_gains(1)
        self.grads_e(D0)
        self.grads_d(U0)
        self.grads_d(P0)
        self.grads_d(P2)
        self.grads_d(P1)
        self.grads_f(Q1)
        self.fold_gains(2)
        if self.R > 1:
            self.fold_gains(3)
        tall = jnp.concatenate([self.nsum[len(self.gain_stages())]] * 16, axis=0).T
        self.gacc[0] = tall
        width = D // Z
        mine = self.gacc[0, pl.ds(pl.multiple_of(self.z * width, 8), width), :]
        mine = jnp.concatenate([mine, jnp.zeros((128 - width, 128), f32)], axis=0).T
        self.gains_grad[...] = mine[0:8]
        self.grads_f(D0)
        self.grads_e(P2)
        self.grads_e(P0)
        self.grads_e(U0)
        self.grads_e(P1)
        self.grads_f(U0)
        for i in (P2, P0, P1):
            self.grads_f(i)
        self.store(0, QP).start()
        out_copy.wait()
        grad_copy.wait()
        for layer in range(LAYERS):
            for t in range(3):
                self.store(layer, t).wait()


def adam(weight, first, second, grad, rate, decay):
    first_new = BETA_ONE * first + (1.0 - BETA_ONE) * grad
    second_new = BETA_TWO * second + (1.0 - BETA_TWO) * grad * grad
    first_fix = 1.0 / (1.0 - BETA_ONE**STEP_COUNT)
    second_fix = 1.0 / (1.0 - BETA_TWO**STEP_COUNT)
    update = first_new * (rate * first_fix) / (jnp.sqrt(second_new * second_fix) + EPS_ADAM)
    return first_new, second_new, weight * (1.0 - rate * decay) - update


def adam_kernel(*refs):
    (block_in, tgrad_in, grads, gains_grad) = refs[:4]
    masters = refs[4:19]
    block_out, tgrad_out = refs[19:21]
    outs = refs[21:]
    rates = (
        2.5 / math.sqrt(D),
        2.5 / math.sqrt(max(4 * D // SEQ, 1)),
        2.5 / math.sqrt(D),
        2.5 / math.sqrt(FF),
        0.5,
    )
    block_out[...] = block_in[...]
    tgrad_out[...] = tgrad_in[...]

    def update(kind, index, grad):
        weight, first, second = (masters[3 * kind + j] for j in range(3))
        new = adam(
            weight[index], first[index], second[index], grad, rates[kind],
            0.1 if kind < 4 else 0.0,
        )
        for j in range(3):
            outs[3 * kind + j][index] = new[j]

    for g in range(GROUPS):
        grad = grads[0, QP, g, 0].astype(f32)
        if g < 3:
            update(0, (0, 0, slice(None), slice(g * D, (g + 1) * D)), grad)
        else:
            update(1, (0, 0), grad)
        update(2, (0, 0, slice(None), slice(g * D, (g + 1) * D)), grads[0, UP, g, 0].astype(f32))
        update(3, (0, g, 0), grads[0, DOWN, g, 0].astype(f32))
    width = masters[12].shape[-1]
    for layer in range(LAYERS):
        update(4, (layer,), gains_grad[2 * layer : 2 * layer + 2, 0:width])


def make_per_device(n_dp, n_fsdp):
    Z, R = n_fsdp, n_dp // UNITS
    UR = D // Z // CORES

    def per_device(
        tokens, cotangent, prefix_len, valid_len,
        qkv_weight, qkv_first, qkv_second,
        proj_weight, proj_first, proj_second,
        up_weight, up_first, up_second,
        down_weight, down_first, down_second,
        norm_gains, gains_first, gains_second,
    ):
        T = tokens.shape[0]
        assert prefix_len.shape == (1,) and T == 4 * BLOCK
        assert Z == 4 and FF // Z // UNITS == UR
        rows4 = lambda w: w.reshape(LAYERS, CORES, UR, w.shape[-1])
        rows5 = lambda w: w.reshape(LAYERS, GROUPS, CORES, UR, D)
        vmem = pltpu.VMEM
        scratch = dict(
            wqp=vmem((LAYERS, Z, CORES, UR, 4 * D), bf16),
            wup=vmem((LAYERS, Z, CORES, UR, FF), bf16),
            wdn=vmem((LAYERS, Z, GROUPS, CORES, UR, D), bf16),
            sq=vmem((UR, 3 * D), f32),
            sp=vmem((UR, D), f32),
            su=vmem((UR, FF), f32),
            sd=vmem((GROUPS, UR, D), f32),
            gslot=vmem((Z, 8, 128), f32),
            gcol=vmem((2 * LAYERS, D, 128), bf16),
            gacc=vmem((2 * LAYERS, D, 128), f32),
            xs=vmem((2 * LAYERS, D, T), f32),
            dy=vmem((D, T), f32),
            an=vmem((LAYERS, D, T), bf16),
            bn=vmem((LAYERS, D, T), bf16),
            qkv=vmem((LAYERS, 3 * D, T), bf16),
            om=vmem((LAYERS, D, T), bf16),
            hid=vmem((LAYERS, FF, T), bf16),
            slope=vmem((LAYERS, FF, T), bf16),
            dqkv=vmem((3 * D, T), bf16),
            dmix=vmem((D, T), bf16),
            dm=vmem((D, T), bf16),
            datt=vmem((D, T), bf16),
            lse=vmem((LAYERS, 8, T), f32),
            stats=vmem((4 * LAYERS, T), f32),
            bias=vmem((5, BLOCK, BLOCK), f32),
            toks=vmem((T, D), bf16),
            cots=vmem((T, D), bf16),
            gb=vmem((3, 2, 2, Z, CORES, UR, D), bf16),
            ra=vmem((4, 2, 2, Z, UR, D), bf16),
            rb1=vmem((4, 2, 2, Z // 2, UR, D), bf16),
            rb2=vmem((4, 2, Z // 2, UR, D), bf16),
            rb=vmem((GROUPS - 1, Z, UR, PAIR), bf16),
            sc=vmem((4, Z, UR, D), bf16),
            rc=vmem((LAYERS, 3, Z - 1, UR, D), bf16),
            fin=vmem((LAYERS, 3, GROUPS, CORES, UR, D), bf16),
            nsum=vmem((5, 8, D), f32),
            nin=vmem((GROUPS + Z + R - 2, 8, D), f32),
        )
        sem = pltpu.SemaphoreType.DMA
        scratch.update(
            zs=sem((1,)),
            zr=sem((Z - 2 + 3 * LAYERS,)),
            gs=sem((3 * LAYERS,)),
            gr=sem((3 * LAYERS, Z - 1)),
            cs=sem((LAYERS,)),
            cr=sem((3 * LAYERS,)),
            rs=sem((len(ITEMS), 6)),
            rr=sem((len(ITEMS), 6)),
            ns=sem((5,)),
            nr=sem((5,)),
            in_sem=sem((2 + 4 * LAYERS,)),
            out_sem=sem((2 + 3 * LAYERS,)),
        )
        if R > 1:
            scratch.update(
                rx=vmem((LAYERS, 3, R - 1, UR, D), bf16),
                rx_out=vmem((LAYERS, 3, UR, D), bf16),
                rxs=sem((len(ITEMS),)),
                rxr=sem((len(ITEMS),)),
            )
        ins = dict(
            tokens=tokens, cotangent=cotangent, prefix=prefix_len, valid=valid_len,
            qkv_w=rows4(qkv_weight), proj_w=rows4(proj_weight), up_w=rows4(up_weight),
            down_w=rows5(down_weight), gains=norm_gains,
        )
        outs = dict(
            block_out=jax.ShapeDtypeStruct((T, D), bf16),
            tokens_grad=jax.ShapeDtypeStruct((T, D), bf16),
            grads_out=jax.ShapeDtypeStruct((LAYERS, 3, GROUPS, CORES, UR, D), bf16),
            gains_grad=jax.ShapeDtypeStruct((8, 128), f32),
        )
        names = list(ins) + list(outs) + list(scratch)
        hbm = pl.BlockSpec(memory_space=pl.ANY)
        smem = pl.BlockSpec(memory_space=pltpu.SMEM)
        local = pl.BlockSpec(memory_space=pltpu.VMEM)

        def kernel(*refs):
            Step(dict(T=T, Z=Z, R=R, UR=UR), dict(zip(names, refs))).run()

        block_mid, tgrad_mid, grads, gains_grad = pl.pallas_call(
            kernel,
            out_shape=list(outs.values()),
            in_specs=[hbm, hbm, smem, smem, hbm, hbm, hbm, hbm, local],
            out_specs=[hbm, hbm, hbm, local],
            scratch_shapes=list(scratch.values()),
            compiler_params=pltpu.CompilerParams(
                collective_id=0, has_side_effects=True, vmem_limit_bytes=63 * 1024 * 1024
            ),
            name="train_step",
        )(*ins.values())

        masters = [
            f(w)
            for f, group in (
                (rows4, (qkv_weight, qkv_first, qkv_second)),
                (rows4, (proj_weight, proj_first, proj_second)),
                (rows4, (up_weight, up_first, up_second)),
                (rows5, (down_weight, down_first, down_second)),
                (lambda w: w, (norm_gains, gains_first, gains_second)),
            )
            for w in group
        ]
        tok_block = pl.BlockSpec((T // 4, D), lambda l, c: (2 * l + c, 0))

        def spec(w):
            if w.ndim == 4:
                return pl.BlockSpec((1, 1, *w.shape[2:]), lambda l, c: (l, c, 0, 0))
            if w.ndim == 5:
                return pl.BlockSpec((1, GROUPS, 1, UR, D), lambda l, c: (l, 0, c, 0, 0))
            return pl.BlockSpec(w.shape, lambda l, c: (0, 0, 0))

        specs = [spec(w) for w in masters]
        done = pl.pallas_call(
            adam_kernel,
            grid=(LAYERS, CORES),
            out_shape=[jax.ShapeDtypeStruct((T, D), bf16)] * 2
            + [jax.ShapeDtypeStruct(w.shape, f32) for w in masters],
            in_specs=[
                tok_block,
                tok_block,
                pl.BlockSpec((1, 3, GROUPS, 1, UR, D), lambda l, c: (l, 0, 0, c, 0, 0)),
                pl.BlockSpec((8, 128), lambda l, c: (0, 0)),
                *specs,
            ],
            out_specs=[tok_block, tok_block, *specs],
            compiler_params=pltpu.CompilerParams(vmem_limit_bytes=62 * 1024 * 1024),
            name="adam",
        )(block_mid, tgrad_mid, grads, gains_grad, *masters)
        shapes = [
            w.shape
            for w in (
                qkv_weight, qkv_first, qkv_second, proj_weight, proj_first, proj_second,
                up_weight, up_first, up_second, down_weight, down_first, down_second,
                norm_gains, gains_first, gains_second,
            )
        ]
        news = [x.reshape(s) for x, s in zip(done[2:], shapes)]
        results = []
        for kind in range(5):
            weight_new, second_new, first_new = news[3 * kind + 2], news[3 * kind + 1], news[3 * kind]
            results += [first_new, second_new, weight_new]
        return (done[0], done[1], *results)

    return per_device


def solution(mesh):
    rows = P(("dp", "fsdp"), None)
    lens = P(("dp", "fsdp"))
    weight = P(None, "fsdp", None)
    gain = P(None, None, "fsdp")
    return jax.shard_map(
        make_per_device(mesh.shape["dp"], mesh.shape["fsdp"]),
        mesh=mesh,
        in_specs=(rows, rows, lens, lens, *([weight] * 12), *([gain] * 3)),
        out_specs=(rows, rows, *([weight] * 12), *([gain] * 3)),
        check_vma=False,
    )
```
